256 devices in a mesh: ctx: 16 (over z_lo, y), traj: 16 (over x, z_hi, core).
Axes of the slice: x: 4, y: 4, z: 8 (z_hi: 2, z_lo: 4; z = z_hi * 4 + z_lo), core: 2. Of those that a mesh axis runs over, the one named last changes fastest.
Arguments:
- queries: bfloat16 [16, 2048, 4096], P('traj', 'ctx')
- out_grad: bfloat16 [16, 2048, 4096], P('traj', 'ctx'), may hold values from -6 to 6
- kv_cache: bfloat16 [32, 16, 16, 8, 1024], P('traj', None, 'ctx')
- learner_of: int32 [32], replicated, may hold values from -1 to 15, as said below
- lengths: int32 [16], replicated, may hold values from 1024 to 2048, as said below
Outputs:
- query_grad: bfloat16 [16, 2048, 4096], P('traj', 'ctx')
- cache_grad: float32 [16, 16, 16, 8, 1024], P('traj', None, 'ctx')
The draws below stay inside these ranges and needn't reach their ends.
Inputs may be any that keep to these rules, and one draw needn't show every extreme that they name: `learner_of`: in each decode group of 2 consecutive trajectories exactly one entry is not -1; these entries name every learner trajectory once. `lengths`: lengths are multiples of 128; some trajectory has all 2048 positions valid and another has the fewest allowed.
All inputs are finite; a program needn't handle non-finite values.
Results may differ from the reference program's by a relative error of at most 0.0061.
Values may be sent and summed in bfloat16 or wider, within the bound.
No kernel may reach another device: no remote copies, remote signals or barrier semaphores. Data moves between devices by JAX's collectives and lax.ppermute only.
A program may use at most 64 MiB of HBM per device.

```python
import math
import jax
import jax.numpy as jnp
from jax import lax

HQ = 32
KVH = 4
HD = 128
PAGE = 8
DEC_DEV = 2
L = 2048
CW = 1024
QW = 4096
KEPT = 16
DEC = 32
N_CTX = 16


def draw_queries(key, part):
    key = jax.random.fold_in(key, 1)
    values = jnp.clip(jax.random.normal(key, (KEPT, L, QW), jnp.float32), -8.0, 8.0)
    return values.astype(jnp.bfloat16)


def draw_kv_cache(key, part):
    key = jax.random.fold_in(key, 2)
    values = jnp.clip(jax.random.normal(key, (DEC, L, CW), jnp.float32), -6.0, 6.0)
    return values.reshape(DEC, L // (PAGE * N_CTX), N_CTX, PAGE, CW).astype(jnp.bfloat16)


def draw_learner_of(key, part):
    key = jax.random.fold_in(key, 4)
    order_key, slot_key = jax.random.split(key)
    targets = jax.random.permutation(order_key, KEPT).astype(jnp.int32)
    slots = jax.random.randint(slot_key, (KEPT,), 0, DEC_DEV).astype(jnp.int32)
    places = jnp.arange(KEPT, dtype=jnp.int32) * DEC_DEV + slots
    return jnp.full((DEC,), -1, jnp.int32).at[places].set(targets)


def draw_lengths(key, part):
    key = jax.random.fold_in(key, 3)
    count_key, index_key, other_key = jax.random.split(key, 3)
    lowest = max(1, L // 256)
    highest = L // 128
    counts = jax.random.randint(count_key, (KEPT,), lowest, highest + 1)
    lengths = counts * 128
    chosen = jax.random.randint(index_key, (), 0, KEPT)
    other = (chosen + 1 + jax.random.randint(other_key, (), 0, KEPT - 1)) % KEPT
    lengths = lengths.at[chosen].set(L)
    lengths = lengths.at[other].set(128 * lowest)
    return lengths.astype(jnp.int32)


def block_levels(own_key, extent, cuts, low, high):
    loudness, own = 1.0, jax.random.fold_in(own_key, 6)
    for position, parts in cuts:
        heights = jnp.exp(jax.random.uniform(jax.random.fold_in(own, position), (parts,), jnp.float32, low / len(cuts), high / len(cuts)))
        loudness = loudness * jnp.repeat(heights, extent[position] // parts).reshape([-1 if axis == position else 1 for axis in range(len(extent))])
    return loudness


def centred(key, extent, scale, reach, cuts=(), kind=jnp.bfloat16):
    drawn = jax.random.normal(key, extent, jnp.float32) * scale
    if len(cuts) > 0:
        drawn = block_levels(key, extent, cuts, -0.22, 0.18) * drawn
    return jnp.clip(drawn, min=-reach, max=reach).astype(kind)


def setup_inputs(seed: int = 0) -> dict:
    splits = jax.random.split(jax.random.key(seed), 6)
    return {
        "queries": draw_queries(jax.random.fold_in(splits[5], 71), 0),
        "out_grad": centred(splits[1], (KEPT, L, QW), 1.0, 6.0, ((0, 16), (1, 16))),
        "kv_cache": draw_kv_cache(jax.random.fold_in(splits[5], 71), 0),
        "learner_of": draw_learner_of(jax.random.fold_in(splits[5], 71), 0),
        "lengths": draw_lengths(jax.random.fold_in(splits[5], 71), 0),
    }


def rounded(values):
    return lax.optimization_barrier(values.astype(jnp.bfloat16)).astype(jnp.float32)

def one_trajectory(inputs):
    query_rows, grad_rows, cache_rows, length = inputs
    total_rows = query_rows.shape[0]
    half_width = KVH * HD
    group_size = HQ // KVH
    score_scale = 1.0 / math.sqrt(HD)
    positions = jnp.arange(total_rows, dtype=jnp.int32)
    masked_grad = jnp.where((positions < length)[:, None], grad_rows, jnp.zeros_like(grad_rows))
    query_heads = query_rows.astype(jnp.float32).reshape(total_rows, KVH, group_size, HD)
    grad_heads = masked_grad.astype(jnp.float32).reshape(total_rows, KVH, group_size, HD)
    key_heads = cache_rows[:, :half_width].astype(jnp.float32).reshape(total_rows, KVH, HD)
    value_heads = cache_rows[:, half_width:].astype(jnp.float32).reshape(total_rows, KVH, HD)
    key_grad = jnp.zeros((total_rows, KVH, HD), jnp.float32)
    value_grad = jnp.zeros((total_rows, KVH, HD), jnp.float32)
    query_blocks = []
    block_size = min(512, total_rows)
    for offset in range(0, total_rows, block_size):
        ending = offset + block_size
        query_part = query_heads[offset:ending]
        grad_part = grad_heads[offset:ending]
        key_part = key_heads[:ending]
        value_part = value_heads[:ending]
        allowed = (positions[:ending][None, :] <= positions[offset:ending][:, None]) & (positions[:ending][None, :] < length)
        scores = jnp.einsum('rkgd,jkd->kgrj', query_part, key_part) * score_scale
        scores = jnp.where(allowed, scores, jnp.float32(-1e+30))
        highest = lax.optimization_barrier(jnp.max(scores, axis=-1, keepdims=True))
        weights = jnp.exp(scores - highest)
        probs = weights / lax.optimization_barrier(jnp.sum(weights, axis=-1, keepdims=True))
        grad_probs = jnp.einsum('rkgd,jkd->kgrj', grad_part, value_part)
        row_sums = lax.optimization_barrier(jnp.sum(probs * grad_probs, axis=-1, keepdims=True))
        score_grad = rounded(probs * (grad_probs - row_sums) * score_scale)
        probs_low = rounded(probs)
        query_blocks.append(jnp.einsum('kgrj,jkd->rkgd', score_grad, key_part))
        key_grad = key_grad.at[:ending].add(jnp.einsum('kgrj,rkgd->jkd', score_grad, query_part))
        value_grad = value_grad.at[:ending].add(jnp.einsum('kgrj,rkgd->jkd', probs_low, grad_part))
    query_grad = jnp.concatenate(query_blocks, axis=0).reshape(total_rows, HQ * HD).astype(jnp.bfloat16)
    both = jnp.concatenate([key_grad.reshape(total_rows, half_width), value_grad.reshape(total_rows, half_width)], axis=1)
    return (query_grad, both.reshape(total_rows // (PAGE * N_CTX), N_CTX, PAGE, 2 * half_width))

def reference(queries, out_grad, kv_cache, learner_of, lengths):
    group_rows = learner_of.reshape(-1, DEC_DEV)
    count_traj = group_rows.shape[0]
    kept_flags = (group_rows >= 0).astype(jnp.int32)
    kept_slots = lax.optimization_barrier(jnp.sum(kept_flags * jnp.arange(DEC_DEV, dtype=jnp.int32)[None, :], axis=1)).astype(jnp.int32)
    group_target = lax.optimization_barrier(jnp.max(group_rows, axis=1)).astype(jnp.int32)
    inverse = jnp.zeros((count_traj,), jnp.int32).at[group_target].set(jnp.arange(count_traj, dtype=jnp.int32))
    source = (inverse * DEC_DEV + kept_slots[inverse]).astype(jnp.int32)
    chosen = kv_cache[source]
    total_rows = queries.shape[1]
    chosen = chosen.reshape(count_traj, total_rows, chosen.shape[-1])
    return lax.map(one_trajectory, (queries, out_grad, chosen, lengths))
```

```python
import functools
import math

import jax
import jax.numpy as jnp
from jax import lax
from jax.experimental import pallas as pl
from jax.experimental.pallas import tpu as pltpu
from jax.sharding import Mesh
from jax.sharding import PartitionSpec as P

HQ = 32
KVH = 4
HD = 128
PAGE = 8
DEC_DEV = 2
GROUP = HQ // KVH
NZ = 4
NY = 4
NT = 16
ROWS = 128
SEQ = 2048
SLOTS = 16
CHUNK = SEQ // NZ
HALF = KVH * HD
WIDE = GROUP * ROWS
SCALE = 1.0 / math.sqrt(HD)
EXP2_SCALE = SCALE * math.log2(math.e)
LOW = -1e30
TRAJ = ("tx", "tz", "tc")
VMEM_LIMIT = 56 * 1024 * 1024

SMEM = pl.BlockSpec(memory_space=pltpu.SMEM)
VMEM = pl.BlockSpec(memory_space=pltpu.VMEM)
ANY = pl.BlockSpec(memory_space=pl.ANY)


def shift_pairs(count, shift):
    return [(i, (i + shift) % count) for i in range(count)]


def kernel_params():
    return pltpu.CompilerParams(vmem_limit_bytes=VMEM_LIMIT)


def split_kernel(meta, q_ref, g_ref, *outs):
    y = meta[1]
    for shift in range(NY):
        base = lax.rem(y + shift, NY) * (GROUP * HD)
        for head in range(GROUP):
            columns = pl.ds(pl.multiple_of(base + head * HD, HD), HD)
            outs[shift][0, head] = q_ref[:, columns]
            outs[shift][1, head] = g_ref[:, columns]


def split_heads(meta, queries, grads):
    piece = jax.ShapeDtypeStruct((2, GROUP, ROWS, HD), jnp.bfloat16)
    return pl.pallas_call(
        split_kernel,
        out_shape=[piece] * NY,
        in_specs=[SMEM, VMEM, VMEM],
        out_specs=[VMEM] * NY,
        compiler_params=kernel_params(),
        cost_estimate=pl.CostEstimate(flops=0, bytes_accessed=4 << 20, transcendentals=0),
        name="split_heads",
    )(meta, queries, grads)


def reorder_kernel(source, in_ref, out_ref):
    for t in range(NT):
        out_ref[t] = in_ref[source[t]]


def reorder(source, pages):
    return pl.pallas_call(
        reorder_kernel,
        out_shape=jax.ShapeDtypeStruct(pages.shape, pages.dtype),
        in_specs=[SMEM, VMEM],
        out_specs=VMEM,
        compiler_params=kernel_params(),
        cost_estimate=pl.CostEstimate(flops=0, bytes_accessed=1 << 19, transcendentals=0),
        name="reorder",
    )(source, pages)


def diagonal_allowed(meta, owner, shift):
    y = meta[1]
    key = lax.broadcasted_iota(jnp.int32, (ROWS, 2 * ROWS), 0)
    row = lax.broadcasted_iota(jnp.int32, (ROWS, 2 * ROWS), 1) & (ROWS - 1)
    key_y = (y + NY - ((key >> 3) & (NY - 1))) & (NY - 1)
    key_position = (key >> 5) * ROWS + (owner * NY + key_y) * PAGE + (key & (PAGE - 1))
    return key_position <= lax.rem(y + NY - shift, NY) * ROWS + row


def tile_scores(chunk, queries, grads, keys, allowed):
    scores = lax.dot_general(
        chunk[:keys, :HD], queries, (((1,), (1,)), ((), ())), preferred_element_type=jnp.float32
    )
    grad_probs = lax.dot_general(
        chunk[:keys, HD:], grads, (((1,), (1,)), ((), ())), preferred_element_type=jnp.float32
    )
    scores = scores * EXP2_SCALE
    last = jnp.where(allowed, scores[keys - ROWS :], LOW)
    if keys > ROWS:
        last = jnp.concatenate([scores[: keys - ROWS], last], axis=0)
    return last, grad_probs


def fold(values, op):
    parts = values.reshape(values.shape[0] // 8, 8, values.shape[1])
    return op(parts, axis=0)


def row_block_active(meta, shift):
    block = meta[0] * NY + lax.rem(meta[1] + NY - shift, NY)
    return block * ROWS < meta[2]


def pair_of(qg_ref, which, pair):
    return qg_ref[which, pl.ds(2 * pair, 2)].reshape(2 * ROWS, HD)


def first_kernel(owners, starts, finishes, meta, *refs):
    count = len(owners)
    qg = refs[:NY]
    chunks = refs[NY : NY + count]
    rest = refs[NY + count :]
    if not starts:
        before, rest = rest[0], rest[1:]
    out = rest[0]
    z = meta[0]
    for zz in range(NZ):

        @pl.when(z == zz)
        def _():
            keys = ROWS * (zz + 1)
            for shift in range(NY):

                @pl.when(row_block_active(meta, shift))
                def _():
                    masks = [
                        diagonal_allowed(meta, lax.rem(z + NZ - o, NZ), shift) for o in owners
                    ]

                    def pair_step(pair, carry):
                        columns = pl.ds(pl.multiple_of(pair * 2 * ROWS, 2 * ROWS), 2 * ROWS)
                        queries = pair_of(qg[shift], 0, pair)
                        grads = pair_of(qg[shift], 1, pair)
                        if starts:
                            high = None
                        else:
                            high = before[shift, 0, :, columns]
                            total = before[shift, 1, :, columns]
                            product = before[shift, 2, :, columns]
                        for chunk, allowed in zip(chunks, masks):
                            scores, grad_probs = tile_scores(
                                chunk, queries, grads, keys, allowed
                            )
                            here = fold(scores, jnp.max)
                            new = here if high is None else jnp.maximum(high, here)
                            weights = jnp.exp2(
                                scores.reshape(keys // 8, 8, 2 * ROWS) - new[None]
                            )
                            sums = jnp.sum(weights, axis=0)
                            products = jnp.sum(
                                weights * grad_probs.reshape(keys // 8, 8, 2 * ROWS), axis=0
                            )
                            if high is None:
                                total, product = sums, products
                            else:
                                factor = jnp.exp2(high - new)
                                total = total * factor + sums
                                product = product * factor + products
                            high = new
                        if finishes:
                            top = jnp.max(high, axis=0, keepdims=True)
                            factor = jnp.exp2(high - top)
                            total = jnp.sum(total * factor, axis=0, keepdims=True)
                            product = jnp.sum(product * factor, axis=0, keepdims=True)
                            shape = (8, 2 * ROWS)
                            out[shift, 0, :, columns] = jnp.broadcast_to(
                                top + jnp.log2(total), shape
                            )
                            out[shift, 1, :, columns] = jnp.broadcast_to(product / total, shape)
                        else:
                            out[shift, 0, :, columns] = high
                            out[shift, 1, :, columns] = total
                            out[shift, 2, :, columns] = product
                        return carry

                    lax.fori_loop(0, GROUP // 2, pair_step, 0)


def first_pass(meta, qg, chunks, owners, before, finishes):
    starts = before is None
    args = [meta, *qg, *chunks] + ([] if starts else [before])
    flops = len(chunks) * 2 * 2 * HD * NY * WIDE * CHUNK // 2
    return pl.pallas_call(
        functools.partial(first_kernel, owners, starts, finishes),
        out_shape=jax.ShapeDtypeStruct((NY, 2 if finishes else 3, 8, WIDE), jnp.float32),
        in_specs=[SMEM] + [VMEM] * (len(args) - 1),
        out_specs=VMEM,
        compiler_params=kernel_params(),
        cost_estimate=pl.CostEstimate(flops=flops, bytes_accessed=3 << 20, transcendentals=0),
        name="first_pass",
    )(*args)


def second_kernel(owner, starts, finishes, meta, *refs):
    qg = refs[:NY]
    chunk, stats = refs[NY], refs[NY + 1]
    rest = refs[NY + 2 :]
    if not starts:
        query_before, rest = rest[0], rest[1:]
    if finishes:
        query_outs, kv_out, rest = rest[:NY], rest[NY], rest[NY + 1 :]
    else:
        query_out, kv_out, rest = rest[0], rest[1], rest[2:]
    probs_ref, score_grad_ref, kv_acc = rest
    z = meta[0]
    kv_acc[...] = jnp.zeros_like(kv_acc)
    for zz in range(NZ):

        @pl.when(z == zz)
        def _():
            keys = ROWS * (zz + 1)
            for shift in range(NY):
                active = row_block_active(meta, shift)

                @pl.when(active)
                def _():
                    allowed = diagonal_allowed(meta, lax.rem(z + NZ - owner, NZ), shift)

                    def pair_step(pair, carry):
                        columns = pl.ds(pl.multiple_of(pair * 2 * ROWS, 2 * ROWS), 2 * ROWS)
                        queries = pair_of(qg[shift], 0, pair)
                        grads = pair_of(qg[shift], 1, pair)
                        scores, grad_probs = tile_scores(chunk, queries, grads, keys, allowed)
                        level = stats[shift, 0, 0:1, columns]
                        row_sum = stats[shift, 1, 0:1, columns]
                        probs = jnp.exp2(scores - level)
                        probs_ref[:keys, columns] = probs.astype(jnp.bfloat16)
                        score_grad_ref[:keys, columns] = (
                            probs * (grad_probs - row_sum)
                        ).astype(jnp.bfloat16)
                        return carry

                    lax.fori_loop(0, GROUP // 2, pair_step, 0)
                    score_grad = score_grad_ref[:keys, :]
                    queries = qg[shift][0].reshape(WIDE, HD)
                    grads = qg[shift][1].reshape(WIDE, HD)
                    kv_acc[:keys, :HD] += jnp.dot(
                        score_grad, queries, preferred_element_type=jnp.float32
                    )
                    kv_acc[:keys, HD:] += jnp.dot(
                        probs_ref[:keys, :], grads, preferred_element_type=jnp.float32
                    )
                    part = lax.dot_general(
                        score_grad,
                        chunk[:keys, :HD],
                        (((0,), (0,)), ((), ())),
                        preferred_element_type=jnp.float32,
                    )
                    if not starts:
                        part = part + query_before[shift]
                    if finishes:
                        query_outs[shift][...] = (
                            (part * SCALE).astype(jnp.bfloat16).reshape(GROUP, ROWS, HD)
                        )
                    else:
                        query_out[shift] = part

                @pl.when(jnp.logical_not(active))
                def _():
                    if finishes:
                        query_outs[shift][...] = jnp.zeros((GROUP, ROWS, HD), jnp.bfloat16)

    kv_out[:, :HD] = (kv_acc[:, :HD] * SCALE).astype(kv_out.dtype)
    kv_out[:, HD:] = kv_acc[:, HD:].astype(kv_out.dtype)


def second_pass(meta, qg, chunk, owner, stats, before, finishes):
    starts = before is None
    args = [meta, *qg, chunk, stats] + ([] if starts else [before])
    if finishes:
        outs = [jax.ShapeDtypeStruct((GROUP, ROWS, HD), jnp.bfloat16)] * NY
    else:
        outs = [jax.ShapeDtypeStruct((NY, WIDE, HD), jnp.float32)]
    kv_type = jnp.float32 if finishes else jnp.bfloat16
    outs = outs + [jax.ShapeDtypeStruct((CHUNK, 2 * HD), kv_type)]
    flops = 5 * 2 * HD * NY * WIDE * CHUNK // 2
    return pl.pallas_call(
        functools.partial(second_kernel, owner, starts, finishes),
        out_shape=outs,
        in_specs=[SMEM] + [VMEM] * (len(args) - 1),
        out_specs=[VMEM] * len(outs),
        scratch_shapes=[
            pltpu.VMEM((CHUNK, WIDE), jnp.bfloat16),
            pltpu.VMEM((CHUNK, WIDE), jnp.bfloat16),
            pltpu.VMEM((CHUNK, 2 * HD), jnp.float32),
        ],
        compiler_params=kernel_params(),
        cost_estimate=pl.CostEstimate(flops=flops, bytes_accessed=6 << 20, transcendentals=0),
        name="second_pass",
    )(*args)


def join_kernel(meta, *refs):
    out = refs[NY]
    for shift in range(NY):
        base = lax.rem(meta[1] + shift, NY) * (GROUP * HD)
        for head in range(GROUP):
            columns = pl.ds(pl.multiple_of(base + head * HD, HD), HD)
            out[:, columns] = refs[shift][head]


def join_heads(meta, pieces):
    return pl.pallas_call(
        join_kernel,
        out_shape=jax.ShapeDtypeStruct((ROWS, HQ * HD), jnp.bfloat16),
        in_specs=[SMEM] + [VMEM] * NY,
        out_specs=VMEM,
        compiler_params=kernel_params(),
        cost_estimate=pl.CostEstimate(flops=0, bytes_accessed=2 << 20, transcendentals=0),
        name="join_heads",
    )(meta, *pieces)


def join_pages_kernel(meta, *refs):
    out = refs[NY]
    for shift in range(NY):
        base = lax.rem(meta[1] + shift, NY) * HD
        for part in range(2):
            columns = pl.ds(pl.multiple_of(base + part * HALF, HD), HD)
            out[:, columns] = refs[shift][:, part * HD : (part + 1) * HD].astype(jnp.float32)


def join_pages(meta, pieces):
    return pl.pallas_call(
        join_pages_kernel,
        out_shape=jax.ShapeDtypeStruct((SLOTS * PAGE, 2 * HALF), jnp.float32),
        in_specs=[SMEM] + [VMEM] * NY,
        out_specs=VMEM,
        compiler_params=kernel_params(),
        cost_estimate=pl.CostEstimate(flops=0, bytes_accessed=1 << 20, transcendentals=0),
        name="join_pages",
    )(meta, *pieces)


def body(queries, out_grad, kv_cache, learner_of, lengths):
    z = lax.axis_index("cz")
    y = lax.axis_index("cy")
    traj = lax.axis_index(TRAJ)
    group_rows = learner_of.reshape(-1, DEC_DEV)
    kept_flags = (group_rows >= 0).astype(jnp.int32)
    kept_slots = jnp.sum(kept_flags * jnp.arange(DEC_DEV, dtype=jnp.int32)[None, :], axis=1)
    group_target = jnp.max(group_rows, axis=1)
    slots = jnp.arange(NT, dtype=jnp.int32)
    source = jnp.sum(
        jnp.where(group_target[None, :] == slots[:, None], slots[None, :], 0), axis=1
    )
    meta = jnp.stack([z, y, lengths[traj], traj]).astype(jnp.int32)

    pages = lax.dynamic_index_in_dim(
        kv_cache.reshape(DEC_DEV, SLOTS, PAGE, 2 * HALF), kept_slots[traj], 0, keepdims=False
    )
    by_shift = []
    for shift in range(NY):
        head = lax.rem(y + shift, NY) * HD
        piece = jnp.concatenate(
            [
                lax.dynamic_slice(pages, (0, 0, head + part * HALF), (SLOTS, PAGE, HD))
                for part in range(2)
            ],
            axis=2,
        )
        if shift:
            piece = lax.ppermute(piece, "cy", shift_pairs(NY, shift))
        by_shift.append(piece)
    own_pages = jnp.stack(by_shift, axis=1).reshape(SLOTS, NY * PAGE, 2 * HD)
    spread = lax.all_to_all(own_pages, TRAJ, 0, 0, tiled=False)
    ordered = reorder(source, spread)
    routed = lax.all_to_all(ordered, TRAJ, 0, 0, tiled=False)
    own_chunk = routed.reshape(CHUNK, 2 * HD)

    pieces = split_heads(meta, queries[0], out_grad[0])
    qg = [pieces[0]] + [
        lax.ppermute(pieces[shift], "cy", shift_pairs(NY, shift)) for shift in range(1, NY)
    ]

    chunks = [own_chunk] + [
        lax.ppermute(own_chunk, "cz", shift_pairs(NZ, shift)) for shift in range(1, NZ)
    ]
    stats = first_pass(meta, qg, [chunks[0]], (0,), None, False)
    stats = first_pass(meta, qg, [chunks[1], chunks[3]], (1, 3), stats, False)
    stats = first_pass(meta, qg, [chunks[2]], (2,), stats, True)

    query_acc, returned = None, []
    for shift in (2, 1, 3):
        query_acc, part = second_pass(meta, qg, chunks[shift], shift, stats, query_acc, False)
        returned.append(lax.ppermute(part, "cz", shift_pairs(NZ, -shift)))
    *query_parts, total = second_pass(meta, qg, chunks[0], 0, stats, query_acc, True)

    query_back = [query_parts[0]] + [
        lax.ppermute(query_parts[shift], "cy", shift_pairs(NY, -shift)) for shift in range(1, NY)
    ]
    query_grad = join_heads(meta, query_back)

    for part in returned:
        total = total + part.astype(jnp.float32)
    total = total.reshape(SLOTS, NY, PAGE, 2 * HD).astype(jnp.bfloat16)
    page_back = []
    for shift in range(NY):
        piece = total[:, shift].reshape(SLOTS * PAGE, 2 * HD)
        if shift:
            piece = lax.ppermute(piece, "cy", shift_pairs(NY, -shift))
        page_back.append(piece)
    cache_grad = join_pages(meta, page_back)
    return (
        query_grad.reshape(1, ROWS, HQ * HD),
        cache_grad.reshape(1, SLOTS, 1, PAGE, 2 * HALF),
    )


def solution(mesh):
    split = Mesh(mesh.devices.reshape(NZ, NY, 4, 2, 2), ("cz", "cy") + TRAJ)
    ctx = ("cz", "cy")
    placed = (
        P(TRAJ, ctx, None),
        P(TRAJ, ctx, None),
        P(TRAJ, None, ctx, None, None),
        P(),
        P(),
    )
    return jax.shard_map(
        body,
        mesh=split,
        in_specs=placed,
        out_specs=(P(TRAJ, ctx, None), P(TRAJ, None, ctx, None, None)),
        check_vma=False,
    )
```

```python
import functools
import math

import jax
import jax.numpy as jnp
from jax import lax
from jax.experimental import pallas as pl
from jax.experimental.pallas import tpu as pltpu
from jax.sharding import Mesh
from jax.sharding import PartitionSpec as P

HQ = 32
KVH = 4
HD = 128
PAGE = 8
DEC_DEV = 2
GROUP = HQ // KVH
NZ = 4
NY = 4
NT = 16
ROWS = 128
SEQ = 2048
SLOTS = 16
CHUNK = SEQ // NZ
PART = CHUNK // NT
HALF = KVH * HD
WIDE = GROUP * ROWS
PAIR = 2 * ROWS
SCALE = 1.0 / math.sqrt(HD)
EXP2_SCALE = SCALE * math.log2(math.e)
LOW = -1e30
TRAJ = ("tx", "tz", "tc")
VMEM_LIMIT = 20 * 1024 * 1024

SMEM = pl.BlockSpec(memory_space=pltpu.SMEM)
VMEM = pl.BlockSpec(memory_space=pltpu.VMEM)
ANY = pl.BlockSpec(memory_space=pl.ANY)


def shift_pairs(count, shift):
    return [(i, (i + shift) % count) for i in range(count)]


def in_vmem(x):
    return pltpu.with_memory_space_constraint(x, pltpu.VMEM)


def call(
    kernel, scalars, arrays, outs, name, aliases=None, scratch=(), staged=(), anchors=(), hbm=False
):
    args = list(scalars) + [x if i in staged else in_vmem(x) for i, x in enumerate(arrays)]
    return pl.pallas_call(
        kernel,
        out_shape=[(jax.ShapeDtypeStruct if hbm else pltpu.VMEM)(*out) for out in outs],
        in_specs=[SMEM] * len(scalars) + [ANY if i in anchors else VMEM for i in range(len(arrays))],
        out_specs=[VMEM] * len(outs),
        scratch_shapes=list(scratch),
        input_output_aliases=aliases or {},
        compiler_params=pltpu.CompilerParams(vmem_limit_bytes=VMEM_LIMIT),
        cost_estimate=pl.CostEstimate(flops=0, bytes_accessed=1024, transcendentals=0),
        name=name,
    )(*args)


def pages_kernel(y_ref, traj_ref, learner, cache, *outs):
    slot = (learner[DEC_DEV * traj_ref[0] + 1] >= 0).astype(jnp.int32)
    for shift in range(NY):
        head = lax.rem(y_ref[0] + shift, NY) * HD
        for part in range(2):
            columns = pl.ds(pl.multiple_of(head + part * HALF, HD), HD)
            outs[shift][:, part * HD : (part + 1) * HD] = cache[slot, :, columns]


def split_kernel(y_ref, q_ref, g_ref, pages, *outs):
    for shift in range(NY):
        base = lax.rem(y_ref[0] + shift, NY) * (GROUP * HD)
        for head in range(GROUP):
            columns = pl.ds(pl.multiple_of(base + head * HD, HD), HD)
            outs[shift][0, head] = q_ref[:, columns]
            outs[shift][1, head] = g_ref[:, columns]


def stack_kernel(p0, p1, p2, p3, out):
    for shift, piece in enumerate((p0, p1, p2, p3)):
        for quarter in range(SLOTS // 4):
            out[quarter * NY + shift] = piece[quarter * PART : (quarter + 1) * PART, :]


def place_kernel(learner, parts, out):
    for group in range(NT):
        target = learner[DEC_DEV * group]
        for i in range(1, DEC_DEV):
            target = jnp.maximum(target, learner[DEC_DEV * group + i])
        out[target] = parts[group]


def pack_kernel(p0, p1, p2, p3, qg):
    for shift, piece in enumerate((p0, p1, p2, p3)):
        qg[shift] = piece[...]


def diagonal_allowed(y, owner, shift):
    key = lax.broadcasted_iota(jnp.int32, (ROWS, PAIR), 0)
    row = lax.broadcasted_iota(jnp.int32, (ROWS, PAIR), 1) & (ROWS - 1)
    key_y = (y + NY - (key >> 5)) & (NY - 1)
    key_position = ((key >> 3) & 3) * ROWS + (owner * NY + key_y) * PAGE + (key & (PAGE - 1))
    return key_position <= lax.rem(y + NY - shift, NY) * ROWS + row


def tile_scores(chunk, queries, grads, keys, allowed):
    scores = lax.dot_general(
        chunk[:keys, :HD], queries, (((1,), (1,)), ((), ())), preferred_element_type=jnp.float32
    )
    grad_probs = lax.dot_general(
        chunk[:keys, HD:], grads, (((1,), (1,)), ((), ())), preferred_element_type=jnp.float32
    )
    scores = scores * EXP2_SCALE
    last = jnp.where(allowed, scores[keys - ROWS :], LOW)
    if keys > ROWS:
        last = jnp.concatenate([scores[: keys - ROWS], last], axis=0)
    return last, grad_probs


def fold(values, op):
    parts = values.reshape(values.shape[0] // 8, 8, values.shape[1])
    return op(parts, axis=0)


def pair_of(qg, shift, which, pair):
    return qg[shift, which, 2 * pair : 2 * pair + 2].reshape(PAIR, HD)


def each_row_block(z_ref, y_ref, traj_ref, lengths, step, otherwise=None):
    z, y = z_ref[0], y_ref[0]
    length = lengths[traj_ref[0]]
    for zz in range(NZ):

        @pl.when(z == zz)
        def _():
            def one(shift, carry):
                block = z * NY + lax.rem(y + NY - shift, NY)
                active = block * ROWS < length

                @pl.when(active)
                def _():
                    step(shift, ROWS * (zz + 1))

                if otherwise is not None:

                    @pl.when(jnp.logical_not(active))
                    def _():
                        otherwise(shift)

                return carry

            lax.fori_loop(0, NY, one, 0)


def first_kernel(owners, starts, finishes, z_ref, y_ref, traj_ref, lengths, qg, *refs):
    chunks = refs[: len(owners)]
    rest = refs[len(owners) :]
    if not starts:
        before, rest = rest[0], rest[1:]
    out = rest[0]

    def step(shift, keys):
        masks = [
            diagonal_allowed(y_ref[0], lax.rem(z_ref[0] + NZ - o, NZ), shift) for o in owners
        ]
        for pair in range(GROUP // 2):
            columns = slice(pair * PAIR, (pair + 1) * PAIR)
            queries = pair_of(qg, shift, 0, pair)
            grads = pair_of(qg, shift, 1, pair)
            high = None
            if not starts:
                high = before[shift, 0, :, columns]
                total = before[shift, 1, :, columns]
                product = before[shift, 2, :, columns]
            for chunk, allowed in zip(chunks, masks):
                scores, grad_probs = tile_scores(chunk, queries, grads, keys, allowed)
                here = fold(scores, jnp.max)
                new = here if high is None else jnp.maximum(high, here)
                weights = jnp.exp2(scores.reshape(keys // 8, 8, PAIR) - new[None])
                sums = jnp.sum(weights, axis=0)
                products = jnp.sum(weights * grad_probs.reshape(keys // 8, 8, PAIR), axis=0)
                if high is None:
                    total, product = sums, products
                else:
                    factor = jnp.exp2(high - new)
                    total = total * factor + sums
                    product = product * factor + products
                high = new
            if finishes:
                top = jnp.max(high, axis=0, keepdims=True)
                factor = jnp.exp2(high - top)
                total = jnp.sum(total * factor, axis=0, keepdims=True)
                product = jnp.sum(product * factor, axis=0, keepdims=True)
                out[shift, 0, :, columns] = jnp.broadcast_to(top + jnp.log2(total), (8, PAIR))
                out[shift, 1, :, columns] = jnp.broadcast_to(product / total, (8, PAIR))
            else:
                out[shift, 0, :, columns] = high
                out[shift, 1, :, columns] = total
                out[shift, 2, :, columns] = product

    each_row_block(z_ref, y_ref, traj_ref, lengths, step)


def first_pass(scalars, qg, chunks, owners, before, finishes):
    starts = before is None
    shape = (NY, 2 if finishes else 3, 8, WIDE)
    return call(
        functools.partial(first_kernel, owners, starts, finishes),
        scalars,
        [qg, *chunks] + ([] if starts else [before]),
        [(shape, jnp.float32)],
        "first_pass",
    )[0]


def second_kernel(owner, starts, finishes, z_ref, y_ref, traj_ref, lengths, qg, chunk, stats, *refs):
    if not starts:
        query_before, refs = refs[0], refs[1:]
    if finishes:
        arrived, refs = refs[0], refs[1:]
    query_out, kv_out, probs_ref, score_grad_ref, kv_acc = refs
    kv_acc[...] = jnp.zeros_like(kv_acc)

    def step(shift, keys):
        allowed = diagonal_allowed(y_ref[0], lax.rem(z_ref[0] + NZ - owner, NZ), shift)
        for pair in range(GROUP // 2):
            columns = slice(pair * PAIR, (pair + 1) * PAIR)
            queries = pair_of(qg, shift, 0, pair)
            grads = pair_of(qg, shift, 1, pair)
            scores, grad_probs = tile_scores(chunk, queries, grads, keys, allowed)
            level = stats[shift, 0, 0:1, columns]
            row_sum = stats[shift, 1, 0:1, columns]
            probs = jnp.exp2(scores - level)
            probs_ref[:keys, columns] = probs.astype(jnp.bfloat16)
            score_grad_ref[:keys, columns] = (probs * (grad_probs - row_sum)).astype(jnp.bfloat16)
        score_grad = score_grad_ref[:keys, :]
        queries = qg[shift, 0].reshape(WIDE, HD)
        grads = qg[shift, 1].reshape(WIDE, HD)
        kv_acc[:keys, :HD] += jnp.dot(score_grad, queries, preferred_element_type=jnp.float32)
        kv_acc[:keys, HD:] += jnp.dot(
            probs_ref[:keys, :], grads, preferred_element_type=jnp.float32
        )
        part = lax.dot_general(
            score_grad,
            chunk[:keys, :HD],
            (((0,), (0,)), ((), ())),
            preferred_element_type=jnp.float32,
        )
        if not starts:
            part = part + query_before[shift]
        if finishes:
            query_out[shift] = (part * SCALE).astype(jnp.bfloat16).reshape(GROUP, ROWS, HD)
        else:
            query_out[shift] = part

    def otherwise(shift):
        query_out[shift] = jnp.zeros((GROUP, ROWS, HD), jnp.bfloat16)

    each_row_block(
        z_ref, y_ref, traj_ref, lengths, step, otherwise if finishes else None
    )
    key_grad = kv_acc[:, :HD] * SCALE
    value_grad = kv_acc[:, HD:]
    if finishes:
        key_grad = key_grad + arrived[:, :HD].astype(jnp.float32)
        value_grad = value_grad + arrived[:, HD:].astype(jnp.float32)
    kv_out[:, :HD] = key_grad.astype(kv_out.dtype)
    kv_out[:, HD:] = value_grad.astype(kv_out.dtype)


def second_pass(scalars, qg, chunk, owner, stats, before, arrived=None):
    starts, finishes = before is None, arrived is not None
    if finishes:
        outs = [((NY, GROUP, ROWS, HD), jnp.bfloat16), ((CHUNK, 2 * HD), jnp.float32)]
    else:
        outs = [((NY, WIDE, HD), jnp.float32), ((CHUNK, 2 * HD), jnp.bfloat16)]
    arrays = [qg, chunk, stats] + ([] if starts else [before]) + ([arrived] if finishes else [])
    aliases = {} if starts or finishes else {len(scalars) + 3: 0}
    return call(
        functools.partial(second_kernel, owner, starts, finishes),
        scalars,
        arrays,
        outs,
        "second_pass",
        aliases,
        [
            pltpu.VMEM((CHUNK, WIDE), jnp.bfloat16),
            pltpu.VMEM((CHUNK, WIDE), jnp.bfloat16),
            pltpu.VMEM((CHUNK, 2 * HD), jnp.float32),
        ],
    )


def join_kernel(y_ref, own, p1, p2, p3, out):
    for shift, piece in enumerate((own, p1, p2, p3)):
        base = lax.rem(y_ref[0] + shift, NY) * (GROUP * HD)
        for head in range(GROUP):
            columns = pl.ds(pl.multiple_of(base + head * HD, HD), HD)
            out[:, columns] = piece[0, head] if shift == 0 else piece[head]


def add_kernel(own, piece, out):
    out[...] = own[...] + piece[...].astype(jnp.float32)


def sum_kernel(own, piece, *outs):
    for shift in range(NY):
        for quarter in range(SLOTS // 4):
            start = (quarter * NY + shift) * PART
            rows = slice(start, start + PART)
            total = own[rows, :] + piece[rows, :].astype(jnp.float32)
            outs[shift][quarter * PART : (quarter + 1) * PART, :] = total.astype(
                outs[shift].dtype
            )


def join_pages_kernel(y_ref, p0, p1, p2, p3, out):
    for shift, piece in enumerate((p0, p1, p2, p3)):
        head = lax.rem(y_ref[0] + shift, NY) * HD
        for part in range(2):
            columns = pl.ds(pl.multiple_of(head + part * HALF, HD), HD)
            out[:, columns] = piece[:, part * HD : (part + 1) * HD].astype(jnp.float32)


def exchange(pieces, sign):
    return [pieces[0]] + [
        lax.ppermute(pieces[shift], "cy", shift_pairs(NY, sign * shift)) for shift in range(1, NY)
    ]


def join(kernel, scalars, arrays, shape, dtype, name):
    return pl.pallas_call(
        kernel,
        out_shape=jax.ShapeDtypeStruct(shape, dtype),
        in_specs=[SMEM] * len(scalars) + [VMEM] * len(arrays),
        out_specs=VMEM,
        compiler_params=pltpu.CompilerParams(vmem_limit_bytes=VMEM_LIMIT),
        cost_estimate=pl.CostEstimate(flops=0, bytes_accessed=1024, transcendentals=0),
        name=name,
    )(*scalars, *[in_vmem(x) for x in arrays])


def body(queries, out_grad, kv_cache, learner_of, lengths):
    z = lax.axis_index("cz").astype(jnp.int32).reshape(1)
    y = lax.axis_index("cy").astype(jnp.int32).reshape(1)
    traj = lax.axis_index(TRAJ).astype(jnp.int32).reshape(1)

    rows = SLOTS * PAGE
    pieces = call(
        pages_kernel,
        [y, traj, learner_of],
        [kv_cache.reshape(DEC_DEV, rows, 2 * HALF)],
        [((rows, 2 * HD), jnp.bfloat16)] * NY,
        "split_pages",
        staged=(0,),
    )
    pieces = exchange(pieces, 1)
    own_pages = call(
        stack_kernel,
        [],
        pieces,
        [((NT, PART, 2 * HD), jnp.bfloat16)],
        "stack_pages",
        hbm=True,
    )[0]
    query_pieces = call(
        split_kernel,
        [y],
        [queries[0], out_grad[0], own_pages],
        [((2, GROUP, ROWS, HD), jnp.bfloat16)] * NY,
        "split_heads",
        staged=(0, 1, 2),
        anchors=(2,),
    )
    query_pieces = exchange(query_pieces, 1)
    spread = lax.all_to_all(own_pages, TRAJ, 0, 0, tiled=False)
    ordered = call(
        place_kernel,
        [learner_of],
        [spread],
        [((NT, PART, 2 * HD), jnp.bfloat16)],
        "place_parts",
    )[0]
    routed = lax.all_to_all(ordered, TRAJ, 0, 0, tiled=False)
    own_chunk = routed.reshape(CHUNK, 2 * HD)
    qg = call(
        pack_kernel,
        [],
        query_pieces,
        [((NY, 2, GROUP, ROWS, HD), jnp.bfloat16)],
        "pack_heads",
    )[0]

    chunks = [own_chunk] + [
        lax.ppermute(own_chunk, "cz", shift_pairs(NZ, shift)) for shift in range(1, NZ)
    ]
    scalars = [z, y, traj, lengths]
    stats = first_pass(scalars, qg, [chunks[0]], (0,), None, False)
    stats = first_pass(scalars, qg, [chunks[1], chunks[3]], (1, 3), stats, False)
    stats = first_pass(scalars, qg, [chunks[2]], (2,), stats, True)

    query_acc, returned = None, []
    for shift in (2, 1, 3):
        query_acc, part = second_pass(scalars, qg, chunks[shift], shift, stats, query_acc)
        returned.append(lax.ppermute(part, "cz", shift_pairs(NZ, -shift)))
    query_parts, own_part = second_pass(
        scalars, qg, chunks[0], 0, stats, query_acc, returned[0]
    )

    query_back = [query_parts[0:1]] + [
        lax.ppermute(query_parts[shift], "cy", shift_pairs(NY, -shift)) for shift in range(1, NY)
    ]
    own_part = call(
        add_kernel,
        [],
        [own_part, returned[2]],
        [((CHUNK, 2 * HD), jnp.float32)],
        "add_part",
    )[0]
    page_parts = call(
        sum_kernel,
        [],
        [own_part, returned[1]],
        [((rows, 2 * HD), jnp.bfloat16)] * NY,
        "sum_parts",
    )
    page_back = exchange(page_parts, -1)
    query_grad = join(join_kernel, [y], query_back, (ROWS, HQ * HD), jnp.bfloat16, "join_heads")
    cache_grad = join(
        join_pages_kernel, [y], page_back, (rows, 2 * HALF), jnp.float32, "join_pages"
    )
    return (
        query_grad.reshape(1, ROWS, HQ * HD),
        cache_grad.reshape(1, SLOTS, 1, PAGE, 2 * HALF),
    )


def solution(mesh):
    split = Mesh(mesh.devices.reshape(NZ, NY, 4, 2, 2), ("cz", "cy") + TRAJ)
    ctx = ("cz", "cy")
    placed = (
        P(TRAJ, ctx, None),
        P(TRAJ, ctx, None),
        P(TRAJ, None, ctx, None, None),
        P(),
        P(),
    )
    return jax.shard_map(
        body,
        mesh=split,
        in_specs=placed,
        out_specs=(P(TRAJ, ctx, None), P(TRAJ, None, ctx, None, None)),
        check_vma=False,
    )
```

```python
import functools
import math

import jax
import jax.numpy as jnp
from jax import lax
from jax.experimental import pallas as pl
from jax.experimental.pallas import tpu as pltpu
from jax.sharding import Mesh
from jax.sharding import PartitionSpec as P

HQ = 32
KVH = 4
HD = 128
PAGE = 8
DEC_DEV = 2
GROUP = HQ // KVH
NZ = 4
NY = 4
NT = 16
ROWS = 128
SEQ = 2048
SLOTS = 16
PLACES = NY
ALL = range(0, PLACES)
CHUNK = SEQ // NZ
PART = CHUNK // NT
HALF = KVH * HD
WIDE = GROUP * ROWS
PAIR = 2 * ROWS
SCALE = 1.0 / math.sqrt(HD)
EXP2_SCALE = SCALE * math.log2(math.e)
LOW = -1e30
TRAJ = ("tx", "tz", "tc")
VMEM_LIMIT = 16 * 1024 * 1024

SMEM = pl.BlockSpec(memory_space=pltpu.SMEM)
VMEM = pl.BlockSpec(memory_space=pltpu.VMEM)
ANY = pl.BlockSpec(memory_space=pl.ANY)


def shift_pairs(count, shift):
    return [(i, (i + shift) % count) for i in range(count)]


def in_vmem(x):
    return pltpu.with_memory_space_constraint(x, pltpu.VMEM)


def call(
    kernel, scalars, arrays, outs, name, aliases=None, scratch=(), staged=(), anchors=(), hbm=False
):
    args = list(scalars) + [x if i in staged else in_vmem(x) for i, x in enumerate(arrays)]
    return pl.pallas_call(
        kernel,
        out_shape=[(jax.ShapeDtypeStruct if hbm else pltpu.VMEM)(*out) for out in outs],
        in_specs=[SMEM] * len(scalars) + [ANY if i in anchors else VMEM for i in range(len(arrays))],
        out_specs=[VMEM] * len(outs),
        scratch_shapes=list(scratch),
        input_output_aliases=aliases or {},
        compiler_params=pltpu.CompilerParams(vmem_limit_bytes=VMEM_LIMIT),
        cost_estimate=pl.CostEstimate(flops=0, bytes_accessed=1024, transcendentals=0),
        name=name,
    )(*args)


def pages_kernel(y_ref, traj_ref, learner, cache, *outs):
    slot = (learner[DEC_DEV * traj_ref[0] + 1] >= 0).astype(jnp.int32)
    for shift in range(NY):
        head = lax.rem(y_ref[0] + shift, NY) * HD
        for part in range(2):
            columns = pl.ds(pl.multiple_of(head + part * HALF, HD), HD)
            outs[shift][:, part * HD : (part + 1) * HD] = cache[slot, :, columns]


def split_kernel(y_ref, q_ref, g_ref, pages, *outs):
    for shift in range(NY):
        base = lax.rem(y_ref[0] + shift, NY) * (GROUP * HD)
        for head in range(GROUP):
            columns = pl.ds(pl.multiple_of(base + head * HD, HD), HD)
            outs[shift][0, head] = q_ref[:, columns]
            outs[shift][1, head] = g_ref[:, columns]


def stack_kernel(p0, p1, p2, p3, out):
    for shift, piece in enumerate((p0, p1, p2, p3)):
        for quarter in range(SLOTS // 4):
            out[quarter * NY + shift] = piece[quarter * PART : (quarter + 1) * PART, :]


def place_kernel(learner, parts, out):
    for group in range(NT):
        target = learner[DEC_DEV * group]
        for i in range(1, DEC_DEV):
            target = jnp.maximum(target, learner[DEC_DEV * group + i])
        out[target] = parts[group]


def gate_kernel(chunk, *refs):
    pass


def pack_kernel(*refs):
    qg, sems = refs[PLACES], refs[PLACES + 1]
    copies = [pltpu.make_async_copy(refs[i], qg.at[i], sems.at[i]) for i in ALL]
    for copy in copies:
        copy.start()
    for copy in copies:
        copy.wait()


def diagonal_allowed(y, owner, place):
    key = lax.broadcasted_iota(jnp.int32, (ROWS, PAIR), 0)
    row = lax.broadcasted_iota(jnp.int32, (ROWS, PAIR), 1) & (ROWS - 1)
    key_y = (y + NY - (key >> 5)) & (NY - 1)
    key_position = ((key >> 3) & 3) * ROWS + (owner * NY + key_y) * PAGE + (key & (PAGE - 1))
    return key_position <= lax.rem(y + NY - place, NY) * ROWS + row


def tile_scores(chunk, queries, grads, keys, allowed):
    scores = lax.dot_general(
        chunk[:keys, :HD], queries, (((1,), (1,)), ((), ())), preferred_element_type=jnp.float32
    )
    grad_probs = lax.dot_general(
        chunk[:keys, HD:], grads, (((1,), (1,)), ((), ())), preferred_element_type=jnp.float32
    )
    scores = scores * EXP2_SCALE
    last = jnp.where(allowed, scores[keys - ROWS :], LOW)
    if keys > ROWS:
        last = jnp.concatenate([scores[: keys - ROWS], last], axis=0)
    return last, grad_probs


def fold(values, op):
    parts = values.reshape(values.shape[0] // 8, 8, values.shape[1])
    return op(parts, axis=0)


def pair_of(qg, shift, which, pair):
    return qg[shift, which, 2 * pair : 2 * pair + 2].reshape(PAIR, HD)


def each_row_block(z_ref, y_ref, traj_ref, lengths, places, step, otherwise=None):
    z, y = z_ref[0], y_ref[0]
    length = lengths[traj_ref[0]]

    def one(place, block, keys):
        active = block * ROWS < length

        @pl.when(active)
        def _():
            step(place, keys)

        if otherwise is not None:

            @pl.when(jnp.logical_not(active))
            def _():
                otherwise(place)

    for zz in range(NZ):

        @pl.when(z == zz)
        def _():
            level = [p for p in places if p < NY]

            def loop(i, carry):
                place = level[0] + (level[-1] - level[0]) // max(1, len(level) - 1) * i
                one(place, z * NY + lax.rem(y + NY - place, NY), ROWS * (zz + 1))
                return carry

            lax.fori_loop(0, len(level), loop, 0)
            if zz == 0 and NY in places:
                one(NY, (NZ - 1) * NY + y, CHUNK)


def first_kernel(owners, starts, finishes, z_ref, y_ref, traj_ref, lengths, qg, *refs):
    count = len(owners)
    chunks, rest = refs[:count], refs[count:]
    if not starts:
        before, rest = rest[0], rest[1:]
    out, weight_outs, mark_outs = rest[0], rest[1 : 1 + count], rest[1 + count :]

    def step(place, keys):
        masks = [
            diagonal_allowed(y_ref[0], lax.rem(z_ref[0] + NZ - o, NZ), place) for o in owners
        ]
        for pair in range(GROUP // 2):
            columns = slice(pair * PAIR, (pair + 1) * PAIR)
            queries = pair_of(qg, place, 0, pair)
            grads = pair_of(qg, place, 1, pair)
            high = None
            if not starts:
                high = before[place, 0, :, columns]
                total = before[place, 1, :, columns]
                product = before[place, 2, :, columns]
            for chunk, allowed, weight_out, mark_out in zip(
                chunks, masks, weight_outs, mark_outs
            ):
                scores, grad_probs = tile_scores(chunk, queries, grads, keys, allowed)
                here = fold(scores, jnp.max)
                new = here if high is None else jnp.maximum(high, here)
                weights = jnp.exp2(scores.reshape(keys // 8, 8, PAIR) - new[None])
                weight_out[place, :keys, columns] = weights.reshape(keys, PAIR).astype(jnp.bfloat16)
                mark_out[place, :, columns] = new
                sums = jnp.sum(weights, axis=0)
                products = jnp.sum(weights * grad_probs.reshape(keys // 8, 8, PAIR), axis=0)
                if high is None:
                    total, product = sums, products
                else:
                    factor = jnp.exp2(high - new)
                    total = total * factor + sums
                    product = product * factor + products
                high = new
            if finishes:
                top = jnp.max(high, axis=0, keepdims=True)
                factor = jnp.exp2(high - top)
                total = jnp.sum(total * factor, axis=0, keepdims=True)
                product = jnp.sum(product * factor, axis=0, keepdims=True)
                out[place, 0, :, columns] = jnp.broadcast_to(top + jnp.log2(total), (8, PAIR))
                out[place, 1, :, columns] = jnp.broadcast_to(product / total, (8, PAIR))
            else:
                out[place, 0, :, columns] = high
                out[place, 1, :, columns] = total
                out[place, 2, :, columns] = product

    each_row_block(z_ref, y_ref, traj_ref, lengths, ALL, step)


def first_pass(scalars, qg, chunks, owners, before, finishes):
    starts, count = before is None, len(owners)
    results = call(
        functools.partial(first_kernel, owners, starts, finishes),
        scalars,
        [qg, *chunks] + ([] if starts else [before]),
        [((PLACES, 2 if finishes else 3, 8, WIDE), jnp.float32)]
        + [((PLACES, CHUNK, WIDE), jnp.bfloat16)] * count
        + [((PLACES, 8, WIDE), jnp.float32)] * count,
        "first_pass",
    )
    return results[0], list(zip(results[1 : 1 + count], results[1 + count :]))


def second_kernel(places, starts, last, added, z_ref, y_ref, traj_ref, lengths, *refs):
    qg, chunk, weights_ref, marks, stats = refs[:5]
    refs = refs[5:]
    if not starts:
        query_before, refs = refs[0], refs[1:]
    more, refs = refs[:added], refs[added:]
    query_out, kv_out, probs_ref, score_grad_ref, kv_acc = refs
    kv_acc[...] = jnp.zeros_like(kv_acc)

    def step(place, keys):
        for pair in range(GROUP // 2):
            columns = slice(pair * PAIR, (pair + 1) * PAIR)
            grads = pair_of(qg, place, 1, pair)
            grad_probs = lax.dot_general(
                chunk[:keys, HD:],
                grads,
                (((1,), (1,)), ((), ())),
                preferred_element_type=jnp.float32,
            )
            row_sum = stats[place, 1, 0:1, columns]
            factor = jnp.exp2(marks[place, :, columns] - stats[place, 0, :, columns])
            weights = weights_ref[place, :keys, columns].astype(jnp.float32)
            probs = (weights.reshape(keys // 8, 8, PAIR) * factor[None]).reshape(keys, PAIR)
            probs_ref[:keys, columns] = probs.astype(jnp.bfloat16)
            score_grad_ref[:keys, columns] = (probs * (grad_probs - row_sum)).astype(jnp.bfloat16)
        score_grad = score_grad_ref[:keys, :]
        part = lax.dot_general(
            chunk[:keys, :HD],
            score_grad,
            (((0,), (0,)), ((), ())),
            preferred_element_type=jnp.float32,
        )
        if not starts:
            part = part + query_before[place]
        if last:
            for head in range(GROUP):
                columns = slice(head * ROWS, (head + 1) * ROWS)
                query_out[place // 2, head] = (part[:, columns] * SCALE).T.astype(jnp.bfloat16)
        else:
            query_out[place] = part
        queries = qg[place, 0].reshape(WIDE, HD)
        grads = qg[place, 1].reshape(WIDE, HD)
        kv_acc[:keys, :HD] += jnp.dot(score_grad, queries, preferred_element_type=jnp.float32)
        kv_acc[:keys, HD:] += jnp.dot(
            probs_ref[:keys, :], grads, preferred_element_type=jnp.float32
        )

    def otherwise(place):
        query_out[place // 2] = jnp.zeros((GROUP, ROWS, HD), jnp.bfloat16)

    each_row_block(
        z_ref, y_ref, traj_ref, lengths, places, step, otherwise if last else None
    )
    for part, scale in ((slice(0, HD), SCALE), (slice(HD, 2 * HD), 1.0)):
        total = kv_acc[:, part] * scale
        for other in more:
            total = total + other[:, part].astype(jnp.float32)
        kv_out[:, part] = total.astype(kv_out.dtype)


def second_pass(scalars, qg, chunk, kept, stats, before, places=ALL, added=()):
    starts, last = before is None, len(places) < PLACES
    if last:
        outs = [((len(places), GROUP, ROWS, HD), jnp.bfloat16), ((CHUNK, 2 * HD), jnp.float32)]
    else:
        outs = [((PLACES, HD, WIDE), jnp.float32), ((CHUNK, 2 * HD), jnp.bfloat16)]
    arrays = [qg, chunk, *kept, stats] + ([] if starts else [before]) + list(added)
    aliases = {} if starts or last else {len(scalars) + 5: 0}
    return call(
        functools.partial(second_kernel, places, starts, last, len(added)),
        scalars,
        arrays,
        outs,
        "second_pass",
        aliases,
        [
            pltpu.VMEM((CHUNK, WIDE), jnp.bfloat16),
            pltpu.VMEM((CHUNK, WIDE), jnp.bfloat16),
            pltpu.VMEM((CHUNK, 2 * HD), jnp.float32),
        ],
    )


def join_kernel(z_ref, y_ref, own, p1, p2, p3, out):
    for shift, piece in enumerate((own, p1, p2, p3)):
        base = lax.rem(y_ref[0] + shift, NY) * (GROUP * HD)
        for head in range(GROUP):
            columns = pl.ds(pl.multiple_of(base + head * HD, HD), HD)
            out[:, columns] = piece[0, head] if shift == 0 else piece[head]


def sum_kernel(y_ref, own, p1, p2, out):
    for shift in range(NY):
        place = lax.rem(y_ref[0] + NY - shift, NY)
        for quarter in range(SLOTS // 4):
            start = (quarter * NY + shift) * PART
            rows = slice(start, start + PART)
            total = own[rows, :]
            for piece in (p1, p2):
                total = total + piece[rows, :].astype(jnp.float32)
            out[place, quarter * PART : (quarter + 1) * PART, :] = total.astype(out.dtype)


def join_pages_kernel(pieces, out):
    for head in range(KVH):
        for part in range(2):
            start = head * HD + part * HALF
            out[:, start : start + HD] = pieces[head, :, part * HD : (part + 1) * HD].astype(
                jnp.float32
            )


def exchange(pieces, sign):
    return [pieces[0]] + [
        lax.ppermute(pieces[shift], "cy", shift_pairs(NY, sign * shift)) for shift in range(1, NY)
    ]


def join(kernel, scalars, arrays, shape, dtype, name):
    return pl.pallas_call(
        kernel,
        out_shape=jax.ShapeDtypeStruct(shape, dtype),
        in_specs=[SMEM] * len(scalars) + [VMEM] * len(arrays),
        out_specs=VMEM,
        compiler_params=pltpu.CompilerParams(vmem_limit_bytes=VMEM_LIMIT),
        cost_estimate=pl.CostEstimate(flops=0, bytes_accessed=1024, transcendentals=0),
        name=name,
    )(*scalars, *[in_vmem(x) for x in arrays])


def body(queries, out_grad, kv_cache, learner_of, lengths):
    z = lax.axis_index("cz").astype(jnp.int32).reshape(1)
    y = lax.axis_index("cy").astype(jnp.int32).reshape(1)
    traj = lax.axis_index(TRAJ).astype(jnp.int32).reshape(1)

    rows = SLOTS * PAGE
    pieces = call(
        pages_kernel,
        [y, traj, learner_of],
        [kv_cache.reshape(DEC_DEV, rows, 2 * HALF)],
        [((rows, 2 * HD), jnp.bfloat16)] * NY,
        "split_pages",
        staged=(0,),
    )
    pieces = exchange(pieces, 1)
    own_pages = call(
        stack_kernel,
        [],
        pieces,
        [((NT, PART, 2 * HD), jnp.bfloat16)],
        "stack_pages",
        hbm=True,
    )[0]
    query_pieces = call(
        split_kernel,
        [y],
        [queries[0], out_grad[0], own_pages],
        [((2, GROUP, ROWS, HD), jnp.bfloat16)] * NY,
        "split_heads",
        staged=(0, 1, 2),
        anchors=(2,),
    )
    query_pieces = exchange(query_pieces, 1)
    spread = lax.all_to_all(own_pages, TRAJ, 0, 0, tiled=False)
    ordered = call(
        place_kernel,
        [learner_of],
        [spread],
        [((NT, PART, 2 * HD), jnp.bfloat16)],
        "place_parts",
    )[0]
    routed = lax.all_to_all(ordered, TRAJ, 0, 0, tiled=False)
    own_chunk = call(
        gate_kernel,
        [],
        [routed.reshape(CHUNK, 2 * HD), *query_pieces[1:]],
        [((CHUNK, 2 * HD), jnp.bfloat16)],
        "gate",
        {0: 0},
        staged=(1, 2, 3),
        anchors=(1, 2, 3),
    )[0]
    qg = call(
        pack_kernel,
        [],
        query_pieces,
        [((PLACES, 2, GROUP, ROWS, HD), jnp.bfloat16)],
        "pack_heads",
        scratch=[pltpu.SemaphoreType.DMA((PLACES,))],
        staged=ALL,
        anchors=ALL,
    )[0]

    chunks = [own_chunk] + [
        lax.ppermute(own_chunk, "cz", shift_pairs(NZ, shift)) for shift in range(1, NZ)
    ]
    scalars = [z, y, traj, lengths]
    stats, kept = None, [None] * NZ
    for shift in (0, 1, 3, 2):
        stats, (kept[shift],) = first_pass(
            scalars, qg, [chunks[shift]], (shift,), stats, shift == 2
        )

    query_acc, returned = None, []
    for shift in (2, 1, 3):
        query_acc, part = second_pass(
            scalars, qg, chunks[shift], kept[shift], stats, query_acc
        )
        returned.append(lax.ppermute(part, "cz", shift_pairs(NZ, -shift)))
    last = (scalars, qg, chunks[0], kept[0], stats, query_acc)
    odd, own_part = second_pass(*last, (1, 3))
    even, own_part = second_pass(*last, (0, 2), (own_part, returned[0]))
    query_back = [even[0:1]] + [
        lax.ppermute(piece, "cy", shift_pairs(NY, -shift))
        for shift, piece in ((1, odd[0]), (2, even[1]), (3, odd[1]))
    ]
    page_parts = call(
        sum_kernel,
        [y],
        [own_part, returned[1], returned[2]],
        [((NY, rows, 2 * HD), jnp.bfloat16)],
        "sum_parts",
    )[0]
    page_back = lax.all_to_all(page_parts, "cy", 0, 0, tiled=False)
    query_grad = join(
        join_kernel, [z, y], query_back, (ROWS, HQ * HD), jnp.bfloat16, "join_heads"
    )
    cache_grad = join(
        join_pages_kernel, [], [page_back], (rows, 2 * HALF), jnp.float32, "join_pages"
    )
    return (
        query_grad.reshape(1, ROWS, HQ * HD),
        cache_grad.reshape(1, SLOTS, 1, PAGE, 2 * HALF),
    )


def solution(mesh):
    split = Mesh(mesh.devices.reshape(NZ, NY, 4, 2, 2), ("cz", "cy") + TRAJ)
    ctx = ("cz", "cy")
    placed = (
        P(TRAJ, ctx, None),
        P(TRAJ, ctx, None),
        P(TRAJ, None, ctx, None, None),
        P(),
        P(),
    )
    return jax.shard_map(
        body,
        mesh=split,
        in_specs=placed,
        out_specs=(P(TRAJ, ctx, None), P(TRAJ, None, ctx, None, None)),
        check_vma=False,
    )
```

```python
import functools
import math

import jax
import jax.numpy as jnp
from jax import lax
from jax.experimental import pallas as pl
from jax.experimental.pallas import tpu as pltpu
from jax.sharding import Mesh
from jax.sharding import PartitionSpec as P

HQ = 32
KVH = 4
HD = 128
PAGE = 8
DEC_DEV = 2
GROUP = HQ // KVH
NZ = 4
NY = 4
NT = 16
ROWS = 128
SEQ = 2048
SLOTS = 16
PLACES = NY
ALL = range(0, PLACES)
CHUNK = SEQ // NZ
PART = CHUNK // NT
HALF = KVH * HD
WIDE = GROUP * ROWS
QUAD = 4 * ROWS
SCALE = 1.0 / math.sqrt(HD)
EXP2_SCALE = SCALE * math.log2(math.e)
LOW = -1e30
TRAJ = ("tx", "tz", "tc")
VMEM_LIMIT = 16 * 1024 * 1024

SMEM = pl.BlockSpec(memory_space=pltpu.SMEM)
VMEM = pl.BlockSpec(memory_space=pltpu.VMEM)
ANY = pl.BlockSpec(memory_space=pl.ANY)


def shift_pairs(count, shift):
    return [(i, (i + shift) % count) for i in range(count)]


def in_vmem(x):
    return pltpu.with_memory_space_constraint(x, pltpu.VMEM)


def call(
    kernel, scalars, arrays, outs, name, aliases=None, scratch=(), staged=(), anchors=(), hbm=False
):
    args = list(scalars) + [x if i in staged else in_vmem(x) for i, x in enumerate(arrays)]
    return pl.pallas_call(
        kernel,
        out_shape=[(jax.ShapeDtypeStruct if hbm else pltpu.VMEM)(*out) for out in outs],
        in_specs=[SMEM] * len(scalars) + [ANY if i in anchors else VMEM for i in range(len(arrays))],
        out_specs=[VMEM] * len(outs),
        scratch_shapes=list(scratch),
        input_output_aliases=aliases or {},
        compiler_params=pltpu.CompilerParams(vmem_limit_bytes=VMEM_LIMIT),
        cost_estimate=pl.CostEstimate(flops=0, bytes_accessed=1024, transcendentals=0),
        name=name,
    )(*args)


def pages_kernel(y_ref, traj_ref, learner, cache, *outs):
    slot = (learner[DEC_DEV * traj_ref[0] + 1] >= 0).astype(jnp.int32)
    for shift in range(NY):
        head = lax.rem(y_ref[0] + shift, NY) * HD
        for part in range(2):
            columns = pl.ds(pl.multiple_of(head + part * HALF, HD), HD)
            outs[shift][:, part * HD : (part + 1) * HD] = cache[slot, :, columns]


def split_kernel(y_ref, q_ref, g_ref, pages, *outs):
    for shift in range(NY):
        base = lax.rem(y_ref[0] + shift, NY) * (GROUP * HD)
        for head in range(GROUP):
            columns = pl.ds(pl.multiple_of(base + head * HD, HD), HD)
            outs[shift][0, head] = q_ref[:, columns]
            outs[shift][1, head] = g_ref[:, columns]


def stack_kernel(p0, p1, p2, p3, out):
    for shift, piece in enumerate((p0, p1, p2, p3)):
        for quarter in range(SLOTS // 4):
            out[quarter * NY + shift] = piece[quarter * PART : (quarter + 1) * PART, :]


def place_kernel(learner, parts, out):
    for group in range(NT):
        target = learner[DEC_DEV * group]
        for i in range(1, DEC_DEV):
            target = jnp.maximum(target, learner[DEC_DEV * group + i])
        out[target] = parts[group]


def gate_kernel(chunk, *refs):
    pass


def pack_kernel(*refs):
    qg, sems = refs[PLACES], refs[PLACES + 1]
    copies = [pltpu.make_async_copy(refs[i], qg.at[i], sems.at[i]) for i in ALL]
    for copy in copies:
        copy.start()
    for copy in copies:
        copy.wait()


def diagonal_allowed(y, owner, place):
    key = lax.broadcasted_iota(jnp.int32, (ROWS, QUAD), 0)
    row = lax.broadcasted_iota(jnp.int32, (ROWS, QUAD), 1) & (ROWS - 1)
    key_y = (y + NY - (key >> 5)) & (NY - 1)
    key_position = ((key >> 3) & 3) * ROWS + (owner * NY + key_y) * PAGE + (key & (PAGE - 1))
    return key_position <= lax.rem(y + NY - place, NY) * ROWS + row


def tile_scores(chunk, queries, grads, keys, allowed):
    scores = lax.dot_general(
        chunk[:keys, :HD], queries, (((1,), (1,)), ((), ())), preferred_element_type=jnp.float32
    )
    grad_probs = lax.dot_general(
        chunk[:keys, HD:], grads, (((1,), (1,)), ((), ())), preferred_element_type=jnp.float32
    )
    scores = scores * EXP2_SCALE
    last = jnp.where(allowed, scores[keys - ROWS :], LOW)
    if keys > ROWS:
        last = jnp.concatenate([scores[: keys - ROWS], last], axis=0)
    return last, grad_probs


def fold(values, op):
    parts = values.reshape(values.shape[0] // 8, 8, values.shape[1])
    return op(parts, axis=0)


def quad_of(qg, place, which, quad):
    return qg[place, which, 4 * quad : 4 * quad + 4].reshape(QUAD, HD)


def each_row_block(z_ref, y_ref, traj_ref, lengths, places, step, otherwise=None):
    z, y = z_ref[0], y_ref[0]
    length = lengths[traj_ref[0]]

    def one(place, block, keys):
        active = block * ROWS < length

        @pl.when(active)
        def _():
            step(place, keys)

        if otherwise is not None:

            @pl.when(jnp.logical_not(active))
            def _():
                otherwise(place)

    for zz in range(NZ):

        @pl.when(z == zz)
        def _():
            level = [p for p in places if p < NY]

            def loop(i, carry):
                place = level[0] + (level[-1] - level[0]) // max(1, len(level) - 1) * i
                one(place, z * NY + lax.rem(y + NY - place, NY), ROWS * (zz + 1))
                return carry

            lax.fori_loop(0, len(level), loop, 0)
            if zz == 0 and NY in places:
                one(NY, (NZ - 1) * NY + y, CHUNK)


def first_kernel(owner, starts, z_ref, y_ref, traj_ref, lengths, qg, chunk, *refs):
    if not starts:
        before, refs = refs[0], refs[1:]
    out, weight_out, mark_out = refs

    def step(place, keys):
        allowed = diagonal_allowed(y_ref[0], lax.rem(z_ref[0] + NZ - owner, NZ), place)
        for quad in range(GROUP // 4):
            columns = slice(quad * QUAD, (quad + 1) * QUAD)
            queries = quad_of(qg, place, 0, quad)
            grads = quad_of(qg, place, 1, quad)
            scores, grad_probs = tile_scores(chunk, queries, grads, keys, allowed)
            new = fold(scores, jnp.max)
            if not starts:
                high = before[place, 0, :, columns]
                new = jnp.maximum(high, new)
            weights = jnp.exp2(scores.reshape(keys // 8, 8, QUAD) - new[None])
            weight_out[place, :keys, columns] = weights.reshape(keys, QUAD).astype(jnp.bfloat16)
            mark_out[place, :, columns] = new
            total = jnp.sum(weights, axis=0)
            product = jnp.sum(weights * grad_probs.reshape(keys // 8, 8, QUAD), axis=0)
            if not starts:
                factor = jnp.exp2(high - new)
                total = before[place, 1, :, columns] * factor + total
                product = before[place, 2, :, columns] * factor + product
            out[place, 0, :, columns] = new
            out[place, 1, :, columns] = total
            out[place, 2, :, columns] = product

    each_row_block(z_ref, y_ref, traj_ref, lengths, ALL, step)


def first_pass(scalars, qg, chunk, owner, before):
    starts = before is None
    stats, *kept = call(
        functools.partial(first_kernel, owner, starts),
        scalars,
        [qg, chunk] + ([] if starts else [before]),
        [
            ((PLACES, 3, 8, WIDE), jnp.float32),
            ((PLACES, CHUNK, WIDE), jnp.bfloat16),
            ((PLACES, 8, WIDE), jnp.float32),
        ],
        "first_pass",
    )
    return stats, kept


def products_of(qg, chunk, place, keys, probs_ref, score_grad_ref, kv_acc):
    score_grad = score_grad_ref[:keys, :]
    part = lax.dot_general(
        chunk[:keys, :HD],
        score_grad,
        (((0,), (0,)), ((), ())),
        preferred_element_type=jnp.float32,
    )
    queries = qg[place, 0].reshape(WIDE, HD)
    grads = qg[place, 1].reshape(WIDE, HD)
    kv_acc[:keys, :HD] += jnp.dot(score_grad, queries, preferred_element_type=jnp.float32)
    kv_acc[:keys, HD:] += jnp.dot(
        probs_ref[:keys, :], grads, preferred_element_type=jnp.float32
    )
    return part


def pass_scratch():
    return [
        pltpu.VMEM((CHUNK, WIDE), jnp.bfloat16),
        pltpu.VMEM((CHUNK, WIDE), jnp.bfloat16),
        pltpu.VMEM((CHUNK, 2 * HD), jnp.float32),
    ]


def bridge_kernel(owner, z_ref, y_ref, traj_ref, lengths, *refs):
    qg, chunk, before, out, query_out, kv_out, probs_ref, score_grad_ref, kv_acc = refs
    kv_acc[...] = jnp.zeros_like(kv_acc)

    def step(place, keys):
        allowed = diagonal_allowed(y_ref[0], lax.rem(z_ref[0] + NZ - owner, NZ), place)
        for quad in range(GROUP // 4):
            columns = slice(quad * QUAD, (quad + 1) * QUAD)
            queries = quad_of(qg, place, 0, quad)
            grads = quad_of(qg, place, 1, quad)
            scores, grad_probs = tile_scores(chunk, queries, grads, keys, allowed)
            high = before[place, 0, :, columns]
            new = jnp.maximum(high, fold(scores, jnp.max))
            weights = jnp.exp2(scores.reshape(keys // 8, 8, QUAD) - new[None])
            grad_probs = grad_probs.reshape(keys // 8, 8, QUAD)
            top = jnp.max(new, axis=0, keepdims=True)
            factor, newer = jnp.exp2(high - top), jnp.exp2(new - top)
            total = before[place, 1, :, columns] * factor + jnp.sum(weights, axis=0) * newer
            product = (
                before[place, 2, :, columns] * factor
                + jnp.sum(weights * grad_probs, axis=0) * newer
            )
            total = jnp.sum(total, axis=0, keepdims=True)
            row_sum = jnp.sum(product, axis=0, keepdims=True) / total
            out[place, 0, :, columns] = jnp.broadcast_to(top + jnp.log2(total), (8, QUAD))
            out[place, 1, :, columns] = jnp.broadcast_to(row_sum, (8, QUAD))
            probs = weights * (newer / total)[None]
            probs_ref[:keys, columns] = probs.reshape(keys, QUAD).astype(jnp.bfloat16)
            score_grad_ref[:keys, columns] = (
                (probs * (grad_probs - row_sum[None])).reshape(keys, QUAD).astype(jnp.bfloat16)
            )
        query_out[place] = products_of(
            qg, chunk, place, keys, probs_ref, score_grad_ref, kv_acc
        )

    each_row_block(z_ref, y_ref, traj_ref, lengths, ALL, step)
    kv_out[:, :HD] = (kv_acc[:, :HD] * SCALE).astype(kv_out.dtype)
    kv_out[:, HD:] = kv_acc[:, HD:].astype(kv_out.dtype)


def bridge_pass(scalars, qg, chunk, owner, before):
    return call(
        functools.partial(bridge_kernel, owner),
        scalars,
        [qg, chunk, before],
        [
            ((PLACES, 2, 8, WIDE), jnp.float32),
            ((PLACES, HD, WIDE), jnp.float32),
            ((CHUNK, 2 * HD), jnp.bfloat16),
        ],
        "bridge_pass",
        scratch=pass_scratch(),
    )


def second_kernel(places, last, added, z_ref, y_ref, traj_ref, lengths, *refs):
    qg, chunk, weights_ref, marks, stats = refs[:5]
    refs = refs[5:]
    query_before, refs = refs[0], refs[1:]
    more, refs = refs[:added], refs[added:]
    query_out, kv_out, probs_ref, score_grad_ref, kv_acc = refs
    kv_acc[...] = jnp.zeros_like(kv_acc)

    def step(place, keys):
        for quad in range(GROUP // 4):
            columns = slice(quad * QUAD, (quad + 1) * QUAD)
            grads = quad_of(qg, place, 1, quad)
            grad_probs = lax.dot_general(
                chunk[:keys, HD:],
                grads,
                (((1,), (1,)), ((), ())),
                preferred_element_type=jnp.float32,
            )
            row_sum = stats[place, 1, 0:1, columns]
            factor = jnp.exp2(marks[place, :, columns] - stats[place, 0, :, columns])
            weights = weights_ref[place, :keys, columns].astype(jnp.float32)
            probs = (weights.reshape(keys // 8, 8, QUAD) * factor[None]).reshape(keys, QUAD)
            probs_ref[:keys, columns] = probs.astype(jnp.bfloat16)
            score_grad_ref[:keys, columns] = (probs * (grad_probs - row_sum)).astype(jnp.bfloat16)
        part = products_of(qg, chunk, place, keys, probs_ref, score_grad_ref, kv_acc)
        part = part + query_before[place]
        if last:
            for head in range(GROUP):
                columns = slice(head * ROWS, (head + 1) * ROWS)
                query_out[place // 2, head] = (part[:, columns] * SCALE).T.astype(jnp.bfloat16)
        else:
            query_out[place] = part

    def otherwise(place):
        query_out[place // 2] = jnp.zeros((GROUP, ROWS, HD), jnp.bfloat16)

    each_row_block(
        z_ref, y_ref, traj_ref, lengths, places, step, otherwise if last else None
    )
    for part, scale in ((slice(0, HD), SCALE), (slice(HD, 2 * HD), 1.0)):
        total = kv_acc[:, part] * scale
        for other in more:
            total = total + other[:, part].astype(jnp.float32)
        kv_out[:, part] = total.astype(kv_out.dtype)


def second_pass(scalars, qg, chunk, kept, stats, before, places=ALL, added=()):
    last = len(places) < PLACES
    if last:
        outs = [((len(places), GROUP, ROWS, HD), jnp.bfloat16), ((CHUNK, 2 * HD), jnp.float32)]
    else:
        outs = [((PLACES, HD, WIDE), jnp.float32), ((CHUNK, 2 * HD), jnp.bfloat16)]
    arrays = [qg, chunk, *kept, stats, before, *added]
    aliases = {} if last else {len(scalars) + 5: 0}
    return call(
        functools.partial(second_kernel, places, last, len(added)),
        scalars,
        arrays,
        outs,
        "second_pass",
        aliases,
        pass_scratch(),
    )


def join_kernel(z_ref, y_ref, own, p1, p2, p3, out):
    for shift, piece in enumerate((own, p1, p2, p3)):
        base = lax.rem(y_ref[0] + shift, NY) * (GROUP * HD)
        for head in range(GROUP):
            columns = pl.ds(pl.multiple_of(base + head * HD, HD), HD)
            out[:, columns] = piece[0, head] if shift == 0 else piece[head]


def sum_kernel(y_ref, own, p1, p2, out):
    for shift in range(NY):
        place = lax.rem(y_ref[0] + NY - shift, NY)
        for quarter in range(SLOTS // 4):
            start = (quarter * NY + shift) * PART
            rows = slice(start, start + PART)
            total = own[rows, :]
            for piece in (p1, p2):
                total = total + piece[rows, :].astype(jnp.float32)
            out[place, quarter * PART : (quarter + 1) * PART, :] = total.astype(out.dtype)


def join_pages_kernel(pieces, out):
    for head in range(KVH):
        for part in range(2):
            start = head * HD + part * HALF
            out[:, start : start + HD] = pieces[head, :, part * HD : (part + 1) * HD].astype(
                jnp.float32
            )


def exchange(pieces, sign):
    return [pieces[0]] + [
        lax.ppermute(pieces[shift], "cy", shift_pairs(NY, sign * shift)) for shift in range(1, NY)
    ]


def join(kernel, scalars, arrays, shape, dtype, name):
    return pl.pallas_call(
        kernel,
        out_shape=jax.ShapeDtypeStruct(shape, dtype),
        in_specs=[SMEM] * len(scalars) + [VMEM] * len(arrays),
        out_specs=VMEM,
        compiler_params=pltpu.CompilerParams(vmem_limit_bytes=VMEM_LIMIT),
        cost_estimate=pl.CostEstimate(flops=0, bytes_accessed=1024, transcendentals=0),
        name=name,
    )(*scalars, *[in_vmem(x) for x in arrays])


def body(queries, out_grad, kv_cache, learner_of, lengths):
    z = lax.axis_index("cz").astype(jnp.int32).reshape(1)
    y = lax.axis_index("cy").astype(jnp.int32).reshape(1)
    traj = lax.axis_index(TRAJ).astype(jnp.int32).reshape(1)

    rows = SLOTS * PAGE
    pieces = call(
        pages_kernel,
        [y, traj, learner_of],
        [kv_cache.reshape(DEC_DEV, rows, 2 * HALF)],
        [((rows, 2 * HD), jnp.bfloat16)] * NY,
        "split_pages",
        staged=(0,),
    )
    pieces = exchange(pieces, 1)
    own_pages = call(
        stack_kernel,
        [],
        pieces,
        [((NT, PART, 2 * HD), jnp.bfloat16)],
        "stack_pages",
        hbm=True,
    )[0]
    query_pieces = call(
        split_kernel,
        [y],
        [queries[0], out_grad[0], own_pages],
        [((2, GROUP, ROWS, HD), jnp.bfloat16)] * NY,
        "split_heads",
        staged=(0, 1, 2),
        anchors=(2,),
    )
    query_pieces = exchange(query_pieces, 1)
    spread = lax.all_to_all(own_pages, TRAJ, 0, 0, tiled=False)
    ordered = call(
        place_kernel,
        [learner_of],
        [spread],
        [((NT, PART, 2 * HD), jnp.bfloat16)],
        "place_parts",
    )[0]
    routed = lax.all_to_all(ordered, TRAJ, 0, 0, tiled=False)
    own_chunk = call(
        gate_kernel,
        [],
        [routed.reshape(CHUNK, 2 * HD), *query_pieces[1:]],
        [((CHUNK, 2 * HD), jnp.bfloat16)],
        "gate",
        {0: 0},
        staged=(1, 2, 3),
        anchors=(1, 2, 3),
    )[0]
    qg = call(
        pack_kernel,
        [],
        query_pieces,
        [((PLACES, 2, GROUP, ROWS, HD), jnp.bfloat16)],
        "pack_heads",
        scratch=[pltpu.SemaphoreType.DMA((PLACES,))],
        staged=ALL,
        anchors=ALL,
    )[0]

    chunks = [own_chunk] + [
        lax.ppermute(own_chunk, "cz", shift_pairs(NZ, shift)) for shift in range(1, NZ)
    ]
    scalars = [z, y, traj, lengths]
    stats, kept = None, [None] * NZ
    for shift in (0, 3, 1):
        stats, kept[shift] = first_pass(scalars, qg, chunks[shift], shift, stats)
    stats, query_acc, part = bridge_pass(scalars, qg, chunks[2], 2, stats)

    returned = [lax.ppermute(part, "cz", shift_pairs(NZ, -2))]
    for shift in (1, 3):
        query_acc, part = second_pass(
            scalars, qg, chunks[shift], kept[shift], stats, query_acc
        )
        returned.append(lax.ppermute(part, "cz", shift_pairs(NZ, -shift)))
    last = (scalars, qg, chunks[0], kept[0], stats, query_acc)
    odd, own_part = second_pass(*last, (1, 3))
    even, own_part = second_pass(*last, (0, 2), (own_part, returned[0]))
    query_back = [even[0:1]] + [
        lax.ppermute(piece, "cy", shift_pairs(NY, -shift))
        for shift, piece in ((1, odd[0]), (2, even[1]), (3, odd[1]))
    ]
    page_parts = call(
        sum_kernel,
        [y],
        [own_part, returned[1], returned[2]],
        [((NY, rows, 2 * HD), jnp.bfloat16)],
        "sum_parts",
    )[0]
    page_back = lax.all_to_all(page_parts, "cy", 0, 0, tiled=False)
    query_grad = join(
        join_kernel, [z, y], query_back, (ROWS, HQ * HD), jnp.bfloat16, "join_heads"
    )
    cache_grad = join(
        join_pages_kernel, [], [page_back], (rows, 2 * HALF), jnp.float32, "join_pages"
    )
    return (
        query_grad.reshape(1, ROWS, HQ * HD),
        cache_grad.reshape(1, SLOTS, 1, PAGE, 2 * HALF),
    )


def solution(mesh):
    split = Mesh(mesh.devices.reshape(NZ, NY, 4, 2, 2), ("cz", "cy") + TRAJ)
    ctx = ("cz", "cy")
    placed = (
        P(TRAJ, ctx, None),
        P(TRAJ, ctx, None),
        P(TRAJ, None, ctx, None, None),
        P(),
        P(),
    )
    return jax.shard_map(
        body,
        mesh=split,
        in_specs=placed,
        out_specs=(P(TRAJ, ctx, None), P(TRAJ, None, ctx, None, None)),
        check_vma=False,
    )
```

```python
import functools
import math

import jax
import jax.numpy as jnp
from jax import lax
from jax.experimental import pallas as pl
from jax.experimental.pallas import tpu as pltpu
from jax.sharding import Mesh
from jax.sharding import PartitionSpec as P

HQ = 32
KVH = 4
HD = 128
PAGE = 8
DEC_DEV = 2
GROUP = HQ // KVH
NZ = 4
NY = 4
NT = 16
ROWS = 128
SEQ = 2048
SLOTS = 16
PLACES = NY
ALL = range(0, PLACES)
CHUNK = SEQ // NZ
PART = CHUNK // NT
HALF = KVH * HD
WIDE = GROUP * ROWS
QUAD = 4 * ROWS
SCALE = 1.0 / math.sqrt(HD)
EXP2_SCALE = SCALE * math.log2(math.e)
LOW = -1e30
TRAJ = ("tx", "tz", "tc")
VMEM_LIMIT = 16 * 1024 * 1024

SMEM = pl.BlockSpec(memory_space=pltpu.SMEM)
VMEM = pl.BlockSpec(memory_space=pltpu.VMEM)
ANY = pl.BlockSpec(memory_space=pl.ANY)
HBM = pl.BlockSpec(memory_space=pltpu.HBM)


def shift_pairs(count, shift):
    return [(i, (i + shift) % count) for i in range(count)]


def in_vmem(x):
    return pltpu.with_memory_space_constraint(x, pltpu.VMEM)


def swap_pairs(other):
    return [(i, i ^ other) for i in range(NZ)]


def in_hbm(x):
    return pltpu.with_memory_space_constraint(x, pltpu.HBM)


def call(
    kernel, scalars, arrays, outs, name, aliases=None, scratch=(), staged=(), anchors=(), far=(), hbm=False
):
    args = list(scalars) + [
        in_hbm(x) if i in far else x if i in staged else in_vmem(x) for i, x in enumerate(arrays)
    ]
    return pl.pallas_call(
        kernel,
        out_shape=[(jax.ShapeDtypeStruct if hbm else pltpu.VMEM)(*out) for out in outs],
        in_specs=[SMEM] * len(scalars) + [
            HBM if i in far else ANY if i in anchors else VMEM for i in range(len(arrays))
        ],
        out_specs=[VMEM] * len(outs),
        scratch_shapes=list(scratch),
        input_output_aliases=aliases or {},
        compiler_params=pltpu.CompilerParams(vmem_limit_bytes=VMEM_LIMIT),
        cost_estimate=pl.CostEstimate(flops=0, bytes_accessed=1024, transcendentals=0),
        name=name,
    )(*args)


def pages_kernel(y_ref, traj_ref, learner_hbm, cache_hbm, *refs):
    outs, (learner, cache, sems) = refs[:NY], refs[NY:]
    copies = [
        pltpu.make_async_copy(learner_hbm, learner, sems.at[0]),
        pltpu.make_async_copy(cache_hbm, cache, sems.at[1]),
    ]
    for copy in copies:
        copy.start()
    for copy in copies:
        copy.wait()
    slot = (learner[DEC_DEV * traj_ref[0] + 1] >= 0).astype(jnp.int32)
    for shift in range(NY):
        head = lax.rem(y_ref[0] + shift, NY) * HD
        for part in range(2):
            columns = pl.ds(pl.multiple_of(head + part * HALF, HD), HD)
            outs[shift][:, part * HD : (part + 1) * HD] = cache[slot, :, columns]


def split_kernel(y_ref, q_hbm, g_hbm, pages, *refs):
    outs, sem = refs[:NY], refs[NY]
    copies = []
    for shift in range(NY):
        base = lax.rem(y_ref[0] + shift, NY) * (GROUP * HD)
        for head in range(GROUP):
            columns = pl.ds(pl.multiple_of(base + head * HD, HD), HD)
            for which, source in enumerate((q_hbm, g_hbm)):
                copies.append(
                    pltpu.make_async_copy(
                        source.at[:, columns],
                        outs[shift].at[which, head],
                        sem.at[shift, which, head],
                    )
                )
    for copy in copies:
        copy.start()
    for copy in copies:
        copy.wait()


def stack_kernel(p0, p1, p2, p3, out):
    for shift, piece in enumerate((p0, p1, p2, p3)):
        for quarter in range(SLOTS // 4):
            out[quarter * NY + shift] = piece[quarter * PART : (quarter + 1) * PART, :]


def place_kernel(learner_hbm, parts, out, learner, sem):
    copy = pltpu.make_async_copy(learner_hbm, learner, sem)
    copy.start()
    copy.wait()
    for group in range(NT):
        target = learner[DEC_DEV * group]
        for i in range(1, DEC_DEV):
            target = jnp.maximum(target, learner[DEC_DEV * group + i])
        out[target] = parts[group]


def gate_kernel(chunk, *refs):
    pass


def pack_kernel(*refs):
    qg, sems = refs[PLACES], refs[PLACES + 1]
    copies = [pltpu.make_async_copy(refs[i], qg.at[i], sems.at[i]) for i in ALL]
    for copy in copies:
        copy.start()
    for copy in copies:
        copy.wait()


def diagonal_allowed(y, owner, place):
    key = lax.broadcasted_iota(jnp.int32, (ROWS, QUAD), 0)
    row = lax.broadcasted_iota(jnp.int32, (ROWS, QUAD), 1) & (ROWS - 1)
    key_y = (y + NY - (key >> 5)) & (NY - 1)
    key_position = ((key >> 3) & 3) * ROWS + (owner * NY + key_y) * PAGE + (key & (PAGE - 1))
    return key_position <= lax.rem(y + NY - place, NY) * ROWS + row


def tile_scores(chunk, queries, grads, keys, allowed):
    scores = lax.dot_general(
        chunk[:keys, :HD], queries, (((1,), (1,)), ((), ())), preferred_element_type=jnp.float32
    )
    grad_probs = lax.dot_general(
        chunk[:keys, HD:], grads, (((1,), (1,)), ((), ())), preferred_element_type=jnp.float32
    )
    scores = scores * EXP2_SCALE
    last = jnp.where(allowed, scores[keys - ROWS :], LOW)
    if keys > ROWS:
        last = jnp.concatenate([scores[: keys - ROWS], last], axis=0)
    return last, grad_probs


def fold(values, op):
    parts = values.reshape(values.shape[0] // 8, 8, values.shape[1])
    return op(parts, axis=0)


def quad_of(qg, place, which, quad):
    return qg[place, which, 4 * quad : 4 * quad + 4].reshape(QUAD, HD)


def each_row_block(meta, places, step, otherwise=None):
    z, y, length = meta[0], meta[1], meta[2]

    def one(place, block, keys):
        active = block * ROWS < length

        @pl.when(active)
        def _():
            step(place, keys)

        if otherwise is not None:

            @pl.when(jnp.logical_not(active))
            def _():
                otherwise(place)

    for zz in range(NZ):

        @pl.when(z == zz)
        def _():
            level = [p for p in places if p < NY]

            def loop(i, carry):
                place = level[0] + (level[-1] - level[0]) // max(1, len(level) - 1) * i
                one(place, z * NY + lax.rem(y + NY - place, NY), ROWS * (zz + 1))
                return carry

            lax.fori_loop(0, len(level), loop, 0)
            if zz == 0 and NY in places:
                one(NY, (NZ - 1) * NY + y, CHUNK)


def first_kernel(owner, starts, meta, qg, chunk, *refs):
    if not starts:
        before, refs = refs[0], refs[1:]
    if starts:
        refs[-1][...] = chunk[...]
    out, weight_out, mark_out = refs[:3]

    def step(place, keys):
        allowed = diagonal_allowed(meta[1], meta[0] ^ owner, place)
        for quad in range(GROUP // 4):
            columns = slice(quad * QUAD, (quad + 1) * QUAD)
            queries = quad_of(qg, place, 0, quad)
            grads = quad_of(qg, place, 1, quad)
            scores, grad_probs = tile_scores(chunk, queries, grads, keys, allowed)
            new = fold(scores, jnp.max)
            if not starts:
                high = before[place, 0, :, columns]
                new = jnp.maximum(high, new)
            weights = jnp.exp2(scores.reshape(keys // 8, 8, QUAD) - new[None])
            weight_out[place, :keys, columns] = weights.reshape(keys, QUAD).astype(jnp.bfloat16)
            mark_out[place, :, columns] = new
            total = jnp.sum(weights, axis=0)
            product = jnp.sum(weights * grad_probs.reshape(keys // 8, 8, QUAD), axis=0)
            if not starts:
                factor = jnp.exp2(high - new)
                total = before[place, 1, :, columns] * factor + total
                product = before[place, 2, :, columns] * factor + product
            out[place, 0, :, columns] = new
            out[place, 1, :, columns] = total
            out[place, 2, :, columns] = product

    each_row_block(meta, ALL, step)


def first_pass(scalars, qg, chunk, owner, before):
    starts = before is None
    stats, weights, mark, *relay = call(
        functools.partial(first_kernel, owner, starts),
        scalars,
        [qg, chunk] + ([] if starts else [before]),
        [
            ((PLACES, 3, 8, WIDE), jnp.float32),
            ((PLACES, CHUNK, WIDE), jnp.bfloat16),
            ((PLACES, 8, WIDE), jnp.float32),
        ]
        + [((CHUNK, 2 * HD), jnp.bfloat16)] * starts,
        "first_pass",
    )
    return stats, (weights, mark), relay


def products_of(qg, chunk, place, keys, probs_ref, score_grad_ref, kv_acc):
    score_grad = score_grad_ref[:keys, :]
    part = lax.dot_general(
        chunk[:keys, :HD],
        score_grad,
        (((0,), (0,)), ((), ())),
        preferred_element_type=jnp.float32,
    )
    queries = qg[place, 0].reshape(WIDE, HD)
    grads = qg[place, 1].reshape(WIDE, HD)
    kv_acc[:keys, :HD] += jnp.dot(score_grad, queries, preferred_element_type=jnp.float32)
    kv_acc[:keys, HD:] += jnp.dot(
        probs_ref[:keys, :], grads, preferred_element_type=jnp.float32
    )
    return part


def pass_scratch():
    return [
        pltpu.VMEM((CHUNK, WIDE), jnp.bfloat16),
        pltpu.VMEM((CHUNK, WIDE), jnp.bfloat16),
        pltpu.VMEM((CHUNK, 2 * HD), jnp.float32),
    ]


def bridge_kernel(owner, meta, *refs):
    qg, chunk, before, out, query_out, kv_out, probs_ref, score_grad_ref, kv_acc = refs
    kv_acc[...] = jnp.zeros_like(kv_acc)

    def step(place, keys):
        allowed = diagonal_allowed(meta[1], meta[0] ^ owner, place)
        for quad in range(GROUP // 4):
            columns = slice(quad * QUAD, (quad + 1) * QUAD)
            queries = quad_of(qg, place, 0, quad)
            grads = quad_of(qg, place, 1, quad)
            scores, grad_probs = tile_scores(chunk, queries, grads, keys, allowed)
            high = before[place, 0, :, columns]
            new = jnp.maximum(high, fold(scores, jnp.max))
            weights = jnp.exp2(scores.reshape(keys // 8, 8, QUAD) - new[None])
            grad_probs = grad_probs.reshape(keys // 8, 8, QUAD)
            top = jnp.max(new, axis=0, keepdims=True)
            factor, newer = jnp.exp2(high - top), jnp.exp2(new - top)
            total = before[place, 1, :, columns] * factor + jnp.sum(weights, axis=0) * newer
            product = (
                before[place, 2, :, columns] * factor
                + jnp.sum(weights * grad_probs, axis=0) * newer
            )
            total = jnp.sum(total, axis=0, keepdims=True)
            row_sum = jnp.sum(product, axis=0, keepdims=True) / total
            out[place, 0, :, columns] = jnp.broadcast_to(top + jnp.log2(total), (8, QUAD))
            out[place, 1, :, columns] = jnp.broadcast_to(row_sum, (8, QUAD))
            probs = weights * (newer / total)[None]
            probs_ref[:keys, columns] = probs.reshape(keys, QUAD).astype(jnp.bfloat16)
            score_grad_ref[:keys, columns] = (
                (probs * (grad_probs - row_sum[None])).reshape(keys, QUAD).astype(jnp.bfloat16)
            )
        query_out[place] = products_of(
            qg, chunk, place, keys, probs_ref, score_grad_ref, kv_acc
        )

    each_row_block(meta, ALL, step)
    kv_out[:, :HD] = (kv_acc[:, :HD] * SCALE).astype(kv_out.dtype)
    kv_out[:, HD:] = kv_acc[:, HD:].astype(kv_out.dtype)


def bridge_pass(scalars, qg, chunk, owner, before):
    return call(
        functools.partial(bridge_kernel, owner),
        scalars,
        [qg, chunk, before],
        [
            ((PLACES, 2, 8, WIDE), jnp.float32),
            ((PLACES, HD, WIDE), jnp.float32),
            ((CHUNK, 2 * HD), jnp.bfloat16),
        ],
        "bridge_pass",
        scratch=pass_scratch(),
    )


def second_kernel(places, last, added, meta, *refs):
    qg, chunk, weights_ref, marks, stats = refs[:5]
    refs = refs[5:]
    query_before, refs = refs[0], refs[1:]
    more, refs = refs[:added], refs[added:]
    query_out, kv_out, probs_ref, score_grad_ref, kv_acc = refs
    kv_acc[...] = jnp.zeros_like(kv_acc)

    def step(place, keys):
        for quad in range(GROUP // 4):
            columns = slice(quad * QUAD, (quad + 1) * QUAD)
            grads = quad_of(qg, place, 1, quad)
            grad_probs = lax.dot_general(
                chunk[:keys, HD:],
                grads,
                (((1,), (1,)), ((), ())),
                preferred_element_type=jnp.float32,
            )
            row_sum = stats[place, 1, 0:1, columns]
            factor = jnp.exp2(marks[place, :, columns] - stats[place, 0, :, columns])
            weights = weights_ref[place, :keys, columns].astype(jnp.float32)
            probs = (weights.reshape(keys // 8, 8, QUAD) * factor[None]).reshape(keys, QUAD)
            probs_ref[:keys, columns] = probs.astype(jnp.bfloat16)
            score_grad_ref[:keys, columns] = (probs * (grad_probs - row_sum)).astype(jnp.bfloat16)
        part = products_of(qg, chunk, place, keys, probs_ref, score_grad_ref, kv_acc)
        part = part + query_before[place]
        if last:
            for head in range(GROUP):
                columns = slice(head * ROWS, (head + 1) * ROWS)
                query_out[place // 2, head] = (part[:, columns] * SCALE).T.astype(jnp.bfloat16)
        else:
            query_out[place] = part

    def otherwise(place):
        query_out[place // 2] = jnp.zeros((GROUP, ROWS, HD), jnp.bfloat16)

    each_row_block(meta, places, step, otherwise if last else None)
    for part, scale in ((slice(0, HD), SCALE), (slice(HD, 2 * HD), 1.0)):
        total = kv_acc[:, part] * scale
        for other in more:
            total = total + other[:, part].astype(jnp.float32)
        kv_out[:, part] = total.astype(kv_out.dtype)


def second_pass(scalars, qg, chunk, kept, stats, before, places=ALL, added=()):
    last = len(places) < PLACES
    if last:
        outs = [((len(places), GROUP, ROWS, HD), jnp.bfloat16), ((CHUNK, 2 * HD), jnp.float32)]
    else:
        outs = [((PLACES, HD, WIDE), jnp.float32), ((CHUNK, 2 * HD), jnp.bfloat16)]
    arrays = [qg, chunk, *kept, stats, before, *added]
    aliases = {} if last else {len(scalars) + 5: 0}
    return call(
        functools.partial(second_kernel, places, last, len(added)),
        scalars,
        arrays,
        outs,
        "second_pass",
        aliases,
        pass_scratch(),
    )


def join_kernel(y_ref, own, p1, p2, p3, out, mark):
    mark[...] = jnp.zeros_like(mark)
    for shift, piece in enumerate((own, p1, p2, p3)):
        base = lax.rem(y_ref[0] + shift, NY) * (GROUP * HD)
        for head in range(GROUP):
            columns = pl.ds(pl.multiple_of(base + head * HD, HD), HD)
            out[:, columns] = piece[0, head] if shift == 0 else piece[head]


def sum_kernel(y_ref, own, p1, p2, out):
    for shift in range(NY):
        place = lax.rem(y_ref[0] + NY - shift, NY)
        for quarter in range(SLOTS // 4):
            start = (quarter * NY + shift) * PART
            rows = slice(start, start + PART)
            total = own[rows, :]
            for piece in (p1, p2):
                total = total + piece[rows, :].astype(jnp.float32)
            out[place, quarter * PART : (quarter + 1) * PART, :] = total.astype(out.dtype)


def join_pages_kernel(pieces, mark, out):
    for head in range(KVH):
        for part in range(2):
            start = head * HD + part * HALF
            out[:, start : start + HD] = pieces[head, :, part * HD : (part + 1) * HD].astype(
                jnp.float32
            )


def exchange(pieces, sign):
    return [pieces[0]] + [
        lax.ppermute(pieces[shift], "cy", shift_pairs(NY, sign * shift)) for shift in range(1, NY)
    ]


def join(kernel, scalars, arrays, shape, dtype, name, marks=False):
    outs = [jax.ShapeDtypeStruct(shape, dtype)]
    if marks:
        outs.append(pltpu.VMEM((8, HD), jnp.float32))
    return pl.pallas_call(
        kernel,
        out_shape=outs,
        in_specs=[SMEM] * len(scalars) + [VMEM] * len(arrays),
        out_specs=[VMEM] * len(outs),
        compiler_params=pltpu.CompilerParams(vmem_limit_bytes=VMEM_LIMIT),
        cost_estimate=pl.CostEstimate(flops=0, bytes_accessed=1024, transcendentals=0),
        name=name,
    )(*scalars, *[in_vmem(x) for x in arrays])


def body(queries, out_grad, kv_cache, learner_of, lengths):
    z = lax.axis_index("cz").astype(jnp.int32).reshape(1)
    y = lax.axis_index("cy").astype(jnp.int32).reshape(1)
    traj = lax.axis_index(TRAJ).astype(jnp.int32).reshape(1)

    scalars = [jnp.stack([z[0], y[0], lengths[traj[0]]])]

    rows = SLOTS * PAGE
    pieces = call(
        pages_kernel,
        [y, traj],
        [learner_of, kv_cache.reshape(DEC_DEV, rows, 2 * HALF)],
        [((rows, 2 * HD), jnp.bfloat16)] * NY,
        "split_pages",
        scratch=[
            pltpu.SMEM((DEC_DEV * NT,), jnp.int32),
            pltpu.VMEM((DEC_DEV, rows, 2 * HALF), jnp.bfloat16),
            pltpu.SemaphoreType.DMA((2,)),
        ],
        far=(0, 1),
    )
    pieces = exchange(pieces, 1)
    own_pages = call(
        stack_kernel,
        [],
        pieces,
        [((NT, PART, 2 * HD), jnp.bfloat16)],
        "stack_pages",
        hbm=True,
    )[0]
    query_pieces = call(
        split_kernel,
        [y],
        [queries[0], out_grad[0], own_pages],
        [((2, GROUP, ROWS, HD), jnp.bfloat16)] * NY,
        "split_heads",
        scratch=[pltpu.SemaphoreType.DMA((NY, 2, GROUP))],
        far=(0, 1),
        staged=(2,),
        anchors=(2,),
    )
    query_pieces = exchange(query_pieces, 1)
    spread = lax.all_to_all(own_pages, TRAJ, 0, 0, tiled=False)
    ordered = call(
        place_kernel,
        [],
        [learner_of, spread],
        [((NT, PART, 2 * HD), jnp.bfloat16)],
        "place_parts",
        scratch=[pltpu.SMEM((DEC_DEV * NT,), jnp.int32), pltpu.SemaphoreType.DMA(())],
        far=(0,),
    )[0]
    routed = lax.all_to_all(ordered, TRAJ, 0, 0, tiled=False)
    own_chunk = call(
        gate_kernel,
        [],
        [routed.reshape(CHUNK, 2 * HD), *query_pieces[1:]],
        [((CHUNK, 2 * HD), jnp.bfloat16)],
        "gate",
        {0: 0},
        staged=(1, 2, 3),
        anchors=(1, 2, 3),
    )[0]
    qg = call(
        pack_kernel,
        [],
        query_pieces,
        [((PLACES, 2, GROUP, ROWS, HD), jnp.bfloat16)],
        "pack_heads",
        scratch=[pltpu.SemaphoreType.DMA((PLACES,))],
        staged=ALL,
        anchors=ALL,
    )[0]

    chunks = [own_chunk, None, None, None]
    for other in (1, 3):
        chunks[other] = lax.ppermute(own_chunk, "cz", swap_pairs(other))
    kept = [None] * NZ
    stats, kept[0], (relay,) = first_pass(scalars, qg, own_chunk, 0, None)
    chunks[2] = lax.ppermute(relay, "cz", swap_pairs(2))
    for other in (1, 3):
        stats, kept[other], _ = first_pass(scalars, qg, chunks[other], other, stats)
    stats, query_acc, part = bridge_pass(scalars, qg, chunks[2], 2, stats)

    returned = [lax.ppermute(part, "cz", swap_pairs(2))]
    for other in (3, 1):
        query_acc, part = second_pass(
            scalars, qg, chunks[other], kept[other], stats, query_acc
        )
        returned.append(lax.ppermute(part, "cz", swap_pairs(other)))
    last = (scalars, qg, chunks[0], kept[0], stats, query_acc)
    odd, own_part = second_pass(*last, (1, 3))
    even, own_part = second_pass(*last, (0, 2), (own_part, returned[0]))
    query_back = [even[0:1]] + [
        lax.ppermute(piece, "cy", shift_pairs(NY, -shift))
        for shift, piece in ((1, odd[0]), (2, even[1]), (3, odd[1]))
    ]
    page_parts = call(
        sum_kernel,
        [y],
        [own_part, returned[1], returned[2]],
        [((NY, rows, 2 * HD), jnp.bfloat16)],
        "sum_parts",
        hbm=True,
    )[0]
    page_back = lax.all_to_all(page_parts, "cy", 0, 0, tiled=False)
    query_grad, mark = join(
        join_kernel, [y], query_back, (ROWS, HQ * HD), jnp.bfloat16, "join_heads", True
    )
    (cache_grad,) = join(
        join_pages_kernel, [], [page_back, mark], (rows, 2 * HALF), jnp.float32, "join_pages"
    )
    return (
        query_grad.reshape(1, ROWS, HQ * HD),
        cache_grad.reshape(1, SLOTS, 1, PAGE, 2 * HALF),
    )


def solution(mesh):
    split = Mesh(mesh.devices.reshape(NZ, NY, 4, 2, 2), ("cz", "cy") + TRAJ)
    ctx = ("cz", "cy")
    placed = (
        P(TRAJ, ctx, None),
        P(TRAJ, ctx, None),
        P(TRAJ, None, ctx, None, None),
        P(),
        P(),
    )
    return jax.shard_map(
        body,
        mesh=split,
        in_specs=placed,
        out_specs=(P(TRAJ, ctx, None), P(TRAJ, None, ctx, None, None)),
        check_vma=False,
    )
```

```python
import functools
import math

import jax
import jax.numpy as jnp
from jax import lax
from jax.experimental import pallas as pl
from jax.experimental.pallas import tpu as pltpu
from jax.sharding import Mesh
from jax.sharding import PartitionSpec as P

HQ = 32
KVH = 4
HD = 128
PAGE = 8
DEC_DEV = 2
GROUP = HQ // KVH
NZ = 4
NY = 4
NT = 16
ROWS = 128
SEQ = 2048
SLOTS = 16
PLACES = NY
ALL = range(0, PLACES)
CHUNK = SEQ // NZ
PART = CHUNK // NT
HALF = KVH * HD
WIDE = GROUP * ROWS
QUAD = 4 * ROWS
SCALE = 1.0 / math.sqrt(HD)
EXP2_SCALE = SCALE * math.log2(math.e)
LOW = -1e30
TRAJ = ("tx", "tz", "tc")
VMEM_LIMIT = 16 * 1024 * 1024

SMEM = pl.BlockSpec(memory_space=pltpu.SMEM)
VMEM = pl.BlockSpec(memory_space=pltpu.VMEM)
ANY = pl.BlockSpec(memory_space=pl.ANY)
HBM = pl.BlockSpec(memory_space=pltpu.HBM)


def shift_pairs(count, shift):
    return [(i, (i + shift) % count) for i in range(count)]


def in_vmem(x):
    return pltpu.with_memory_space_constraint(x, pltpu.VMEM)


def swap_pairs(other):
    return [(i, i ^ other) for i in range(NZ)]


def in_hbm(x):
    return pltpu.with_memory_space_constraint(x, pltpu.HBM)


def call(
    kernel, scalars, arrays, outs, name, aliases=None, scratch=(), staged=(), anchors=(), far=(), hbm=False
):
    args = list(scalars) + [
        in_hbm(x) if i in far else x if i in staged else in_vmem(x) for i, x in enumerate(arrays)
    ]
    return pl.pallas_call(
        kernel,
        out_shape=[(jax.ShapeDtypeStruct if hbm else pltpu.VMEM)(*out) for out in outs],
        in_specs=[SMEM] * len(scalars) + [
            HBM if i in far else ANY if i in anchors else VMEM for i in range(len(arrays))
        ],
        out_specs=[VMEM] * len(outs),
        scratch_shapes=list(scratch),
        input_output_aliases=aliases or {},
        compiler_params=pltpu.CompilerParams(vmem_limit_bytes=VMEM_LIMIT),
        cost_estimate=pl.CostEstimate(flops=0, bytes_accessed=1024, transcendentals=0),
        name=name,
    )(*args)


def pages_kernel(y_ref, traj_ref, learner_hbm, cache_hbm, *refs):
    outs, (learner, cache, sems) = refs[:NY], refs[NY:]
    copies = [
        pltpu.make_async_copy(learner_hbm, learner, sems.at[0]),
        pltpu.make_async_copy(cache_hbm, cache, sems.at[1]),
    ]
    for copy in copies:
        copy.start()
    for copy in copies:
        copy.wait()
    slot = (learner[DEC_DEV * traj_ref[0] + 1] >= 0).astype(jnp.int32)
    for shift in range(NY):
        head = lax.rem(y_ref[0] + shift, NY) * HD
        for part in range(2):
            columns = pl.ds(pl.multiple_of(head + part * HALF, HD), HD)
            outs[shift][:, part * HD : (part + 1) * HD] = cache[slot, :, columns]


def split_kernel(y_ref, q_hbm, g_hbm, pages, *refs):
    outs, sem = refs[:NY], refs[NY]
    copies = []
    for shift in range(NY):
        base = lax.rem(y_ref[0] + shift, NY) * (GROUP * HD)
        for head in range(GROUP):
            columns = pl.ds(pl.multiple_of(base + head * HD, HD), HD)
            for which, source in enumerate((q_hbm, g_hbm)):
                copies.append(
                    pltpu.make_async_copy(
                        source.at[:, columns],
                        outs[shift].at[which, head],
                        sem.at[shift, which, head],
                    )
                )
    for copy in copies:
        copy.start()
    for copy in copies:
        copy.wait()


def stack_kernel(p0, p1, p2, p3, out):
    for shift, piece in enumerate((p0, p1, p2, p3)):
        for quarter in range(SLOTS // 4):
            out[quarter * NY + shift] = piece[quarter * PART : (quarter + 1) * PART, :]


def place_kernel(learner_hbm, parts, out, learner, sem):
    copy = pltpu.make_async_copy(learner_hbm, learner, sem)
    copy.start()
    copy.wait()
    for group in range(NT):
        target = learner[DEC_DEV * group]
        for i in range(1, DEC_DEV):
            target = jnp.maximum(target, learner[DEC_DEV * group + i])
        out[target] = parts[group]


def gate_kernel(chunk, *refs):
    pass


def pack_kernel(*refs):
    qg, sems = refs[PLACES], refs[PLACES + 1]
    copies = [pltpu.make_async_copy(refs[i], qg.at[i], sems.at[i]) for i in ALL]
    for copy in copies:
        copy.start()
    for copy in copies:
        copy.wait()


def diagonal_allowed(y, owner, place):
    key = lax.broadcasted_iota(jnp.int32, (ROWS, QUAD), 0)
    row = lax.broadcasted_iota(jnp.int32, (ROWS, QUAD), 1) & (ROWS - 1)
    key_y = (y + NY - (key >> 5)) & (NY - 1)
    key_position = ((key >> 3) & 3) * ROWS + (owner * NY + key_y) * PAGE + (key & (PAGE - 1))
    return key_position <= lax.rem(y + NY - place, NY) * ROWS + row


def tile_scores(chunk, queries, grads, keys, allowed):
    scores = lax.dot_general(
        chunk[:keys, :HD], queries, (((1,), (1,)), ((), ())), preferred_element_type=jnp.float32
    )
    grad_probs = lax.dot_general(
        chunk[:keys, HD:], grads, (((1,), (1,)), ((), ())), preferred_element_type=jnp.float32
    )
    scores = scores * EXP2_SCALE
    last = jnp.where(allowed, scores[keys - ROWS :], LOW)
    if keys > ROWS:
        last = jnp.concatenate([scores[: keys - ROWS], last], axis=0)
    return last, grad_probs


def fold(values, op):
    parts = values.reshape(values.shape[0] // 8, 8, values.shape[1])
    return op(parts, axis=0)


def quad_of(qg, place, which, quad):
    return qg[place, which, 4 * quad : 4 * quad + 4].reshape(QUAD, HD)


def each_row_block(meta, places, step, otherwise=None):
    z, y, length = meta[0], meta[1], meta[2]

    def one(place, block, keys):
        active = block * ROWS < length

        @pl.when(active)
        def _():
            step(place, keys)

        if otherwise is not None:

            @pl.when(jnp.logical_not(active))
            def _():
                otherwise(place)

    for zz in range(NZ):

        @pl.when(z == zz)
        def _():
            level = [p for p in places if p < NY]

            def loop(i, carry):
                place = level[0] + (level[-1] - level[0]) // max(1, len(level) - 1) * i
                one(place, z * NY + lax.rem(y + NY - place, NY), ROWS * (zz + 1))
                return carry

            lax.fori_loop(0, len(level), loop, 0)
            if zz == 0 and NY in places:
                one(NY, (NZ - 1) * NY + y, CHUNK)


def first_kernel(owner, starts, meta, qg, chunk, *refs):
    if not starts:
        before, refs = refs[0], refs[1:]
    out, weight_out, mark_out = refs

    def step(place, keys):
        allowed = diagonal_allowed(meta[1], meta[0] ^ owner, place)
        for quad in range(GROUP // 4):
            columns = slice(quad * QUAD, (quad + 1) * QUAD)
            queries = quad_of(qg, place, 0, quad)
            grads = quad_of(qg, place, 1, quad)
            scores, grad_probs = tile_scores(chunk, queries, grads, keys, allowed)
            new = fold(scores, jnp.max)
            if not starts:
                high = before[place, 0, :, columns]
                new = jnp.maximum(high, new)
            weights = jnp.exp2(scores.reshape(keys // 8, 8, QUAD) - new[None])
            weight_out[place, :keys, columns] = weights.reshape(keys, QUAD).astype(jnp.bfloat16)
            mark_out[place, :, columns] = new
            total = jnp.sum(weights, axis=0)
            product = jnp.sum(weights * grad_probs.reshape(keys // 8, 8, QUAD), axis=0)
            if not starts:
                factor = jnp.exp2(high - new)
                total = before[place, 1, :, columns] * factor + total
                product = before[place, 2, :, columns] * factor + product
            out[place, 0, :, columns] = new
            out[place, 1, :, columns] = total
            out[place, 2, :, columns] = product

    each_row_block(meta, ALL, step)


def first_pass(scalars, qg, chunk, owner, before):
    starts = before is None
    stats, *kept = call(
        functools.partial(first_kernel, owner, starts),
        scalars,
        [qg, chunk] + ([] if starts else [before]),
        [
            ((PLACES, 3, 8, WIDE), jnp.float32),
            ((PLACES, CHUNK, WIDE), jnp.bfloat16),
            ((PLACES, 8, WIDE), jnp.float32),
        ],
        "first_pass",
    )
    return stats, kept


def products_of(qg, chunk, place, keys, probs_ref, score_grad_ref, kv_acc):
    score_grad = score_grad_ref[:keys, :]
    part = lax.dot_general(
        chunk[:keys, :HD],
        score_grad,
        (((0,), (0,)), ((), ())),
        preferred_element_type=jnp.float32,
    )
    queries = qg[place, 0].reshape(WIDE, HD)
    grads = qg[place, 1].reshape(WIDE, HD)
    kv_acc[:keys, :HD] += jnp.dot(score_grad, queries, preferred_element_type=jnp.float32)
    kv_acc[:keys, HD:] += jnp.dot(
        probs_ref[:keys, :], grads, preferred_element_type=jnp.float32
    )
    return part


def pass_scratch():
    return [
        pltpu.VMEM((CHUNK, WIDE), jnp.bfloat16),
        pltpu.VMEM((CHUNK, WIDE), jnp.bfloat16),
        pltpu.VMEM((CHUNK, 2 * HD), jnp.float32),
    ]


def bridge_kernel(owner, meta, *refs):
    qg, chunk, before, out, query_out, kv_out, probs_ref, score_grad_ref, kv_acc = refs
    kv_acc[...] = jnp.zeros_like(kv_acc)

    def step(place, keys):
        allowed = diagonal_allowed(meta[1], meta[0] ^ owner, place)
        for quad in range(GROUP // 4):
            columns = slice(quad * QUAD, (quad + 1) * QUAD)
            queries = quad_of(qg, place, 0, quad)
            grads = quad_of(qg, place, 1, quad)
            scores, grad_probs = tile_scores(chunk, queries, grads, keys, allowed)
            high = before[place, 0, :, columns]
            new = jnp.maximum(high, fold(scores, jnp.max))
            weights = jnp.exp2(scores.reshape(keys // 8, 8, QUAD) - new[None])
            grad_probs = grad_probs.reshape(keys // 8, 8, QUAD)
            top = jnp.max(new, axis=0, keepdims=True)
            factor, newer = jnp.exp2(high - top), jnp.exp2(new - top)
            total = before[place, 1, :, columns] * factor + jnp.sum(weights, axis=0) * newer
            product = (
                before[place, 2, :, columns] * factor
                + jnp.sum(weights * grad_probs, axis=0) * newer
            )
            total = jnp.sum(total, axis=0, keepdims=True)
            row_sum = jnp.sum(product, axis=0, keepdims=True) / total
            out[place, 0, :, columns] = jnp.broadcast_to(top + jnp.log2(total), (8, QUAD))
            out[place, 1, :, columns] = jnp.broadcast_to(row_sum, (8, QUAD))
            probs = weights * (newer / total)[None]
            probs_ref[:keys, columns] = probs.reshape(keys, QUAD).astype(jnp.bfloat16)
            score_grad_ref[:keys, columns] = (
                (probs * (grad_probs - row_sum[None])).reshape(keys, QUAD).astype(jnp.bfloat16)
            )
        query_out[place] = products_of(
            qg, chunk, place, keys, probs_ref, score_grad_ref, kv_acc
        )

    each_row_block(meta, ALL, step)
    kv_out[:, :HD] = (kv_acc[:, :HD] * SCALE).astype(kv_out.dtype)
    kv_out[:, HD:] = kv_acc[:, HD:].astype(kv_out.dtype)


def bridge_pass(scalars, qg, chunk, owner, before):
    return call(
        functools.partial(bridge_kernel, owner),
        scalars,
        [qg, chunk, before],
        [
            ((PLACES, 2, 8, WIDE), jnp.float32),
            ((PLACES, HD, WIDE), jnp.float32),
            ((CHUNK, 2 * HD), jnp.bfloat16),
        ],
        "bridge_pass",
        scratch=pass_scratch(),
    )


def second_kernel(places, last, added, meta, *refs):
    qg, chunk, weights_ref, marks, stats = refs[:5]
    refs = refs[5:]
    query_before, refs = refs[0], refs[1:]
    more, refs = refs[:added], refs[added:]
    query_out, kv_out, probs_ref, score_grad_ref, kv_acc = refs
    kv_acc[...] = jnp.zeros_like(kv_acc)

    def step(place, keys):
        for quad in range(GROUP // 4):
            columns = slice(quad * QUAD, (quad + 1) * QUAD)
            grads = quad_of(qg, place, 1, quad)
            grad_probs = lax.dot_general(
                chunk[:keys, HD:],
                grads,
                (((1,), (1,)), ((), ())),
                preferred_element_type=jnp.float32,
            )
            row_sum = stats[place, 1, 0:1, columns]
            factor = jnp.exp2(marks[place, :, columns] - stats[place, 0, :, columns])
            weights = weights_ref[place, :keys, columns].astype(jnp.float32)
            probs = (weights.reshape(keys // 8, 8, QUAD) * factor[None]).reshape(keys, QUAD)
            probs_ref[:keys, columns] = probs.astype(jnp.bfloat16)
            score_grad_ref[:keys, columns] = (probs * (grad_probs - row_sum)).astype(jnp.bfloat16)
        part = products_of(qg, chunk, place, keys, probs_ref, score_grad_ref, kv_acc)
        part = part + query_before[place]
        if last:
            for head in range(GROUP):
                columns = slice(head * ROWS, (head + 1) * ROWS)
                query_out[place // 2, head] = (part[:, columns] * SCALE).T.astype(jnp.bfloat16)
        else:
            query_out[place] = part

    def otherwise(place):
        query_out[place // 2] = jnp.zeros((GROUP, ROWS, HD), jnp.bfloat16)

    each_row_block(meta, places, step, otherwise if last else None)
    for part, scale in ((slice(0, HD), SCALE), (slice(HD, 2 * HD), 1.0)):
        total = kv_acc[:, part] * scale
        for other in more:
            total = total + other[:, part].astype(jnp.float32)
        kv_out[:, part] = total.astype(kv_out.dtype)


def second_pass(scalars, qg, chunk, kept, stats, before, places=ALL, added=()):
    last = len(places) < PLACES
    if last:
        outs = [((len(places), GROUP, ROWS, HD), jnp.bfloat16), ((CHUNK, 2 * HD), jnp.float32)]
    else:
        outs = [((PLACES, HD, WIDE), jnp.float32), ((CHUNK, 2 * HD), jnp.bfloat16)]
    arrays = [qg, chunk, *kept, stats, before, *added]
    aliases = {} if last else {len(scalars) + 5: 0}
    return call(
        functools.partial(second_kernel, places, last, len(added)),
        scalars,
        arrays,
        outs,
        "second_pass",
        aliases,
        pass_scratch(),
    )


def join_kernel(y_ref, own, p1, p2, p3, out, mark):
    mark[...] = jnp.zeros_like(mark)
    for shift, piece in enumerate((own, p1, p2, p3)):
        base = lax.rem(y_ref[0] + shift, NY) * (GROUP * HD)
        for head in range(GROUP):
            columns = pl.ds(pl.multiple_of(base + head * HD, HD), HD)
            out[:, columns] = piece[0, head] if shift == 0 else piece[head]


def sum_kernel(y_ref, own, p1, p2, out):
    for shift in range(NY):
        place = lax.rem(y_ref[0] + NY - shift, NY)
        for quarter in range(SLOTS // 4):
            start = (quarter * NY + shift) * PART
            rows = slice(start, start + PART)
            total = own[rows, :]
            for piece in (p1, p2):
                total = total + piece[rows, :].astype(jnp.float32)
            out[place, quarter * PART : (quarter + 1) * PART, :] = total.astype(out.dtype)


def join_pages_kernel(pieces, mark, out):
    for head in range(KVH):
        for part in range(2):
            start = head * HD + part * HALF
            out[:, start : start + HD] = pieces[head, :, part * HD : (part + 1) * HD].astype(
                jnp.float32
            )


def exchange(pieces, sign):
    return [pieces[0]] + [
        lax.ppermute(pieces[shift], "cy", shift_pairs(NY, sign * shift)) for shift in range(1, NY)
    ]


def join(kernel, scalars, arrays, shape, dtype, name, marks=False):
    outs = [jax.ShapeDtypeStruct(shape, dtype)]
    if marks:
        outs.append(pltpu.VMEM((8, HD), jnp.float32))
    return pl.pallas_call(
        kernel,
        out_shape=outs,
        in_specs=[SMEM] * len(scalars) + [VMEM] * len(arrays),
        out_specs=[VMEM] * len(outs),
        compiler_params=pltpu.CompilerParams(vmem_limit_bytes=VMEM_LIMIT),
        cost_estimate=pl.CostEstimate(flops=0, bytes_accessed=1024, transcendentals=0),
        name=name,
    )(*scalars, *[in_vmem(x) for x in arrays])


def body(queries, out_grad, kv_cache, learner_of, lengths):
    z = lax.axis_index("cz").astype(jnp.int32).reshape(1)
    y = lax.axis_index("cy").astype(jnp.int32).reshape(1)
    traj = lax.axis_index(TRAJ).astype(jnp.int32).reshape(1)

    scalars = [jnp.stack([z[0], y[0], lengths[traj[0]]])]

    rows = SLOTS * PAGE
    pieces = call(
        pages_kernel,
        [y, traj],
        [learner_of, kv_cache.reshape(DEC_DEV, rows, 2 * HALF)],
        [((rows, 2 * HD), jnp.bfloat16)] * NY,
        "split_pages",
        scratch=[
            pltpu.SMEM((DEC_DEV * NT,), jnp.int32),
            pltpu.VMEM((DEC_DEV, rows, 2 * HALF), jnp.bfloat16),
            pltpu.SemaphoreType.DMA((2,)),
        ],
        far=(0, 1),
    )
    pieces = exchange(pieces, 1)
    own_pages = call(
        stack_kernel,
        [],
        pieces,
        [((NT, PART, 2 * HD), jnp.bfloat16)],
        "stack_pages",
        hbm=True,
    )[0]
    query_pieces = call(
        split_kernel,
        [y],
        [queries[0], out_grad[0], own_pages],
        [((2, GROUP, ROWS, HD), jnp.bfloat16)] * NY,
        "split_heads",
        scratch=[pltpu.SemaphoreType.DMA((NY, 2, GROUP))],
        far=(0, 1),
        staged=(2,),
        anchors=(2,),
    )
    query_pieces = exchange(query_pieces, 1)
    spread = lax.all_to_all(own_pages, TRAJ, 0, 0, tiled=False)
    ordered = call(
        place_kernel,
        [],
        [learner_of, spread],
        [((NT, PART, 2 * HD), jnp.bfloat16)],
        "place_parts",
        scratch=[pltpu.SMEM((DEC_DEV * NT,), jnp.int32), pltpu.SemaphoreType.DMA(())],
        far=(0,),
    )[0]
    routed = lax.all_to_all(ordered, TRAJ, 0, 0, tiled=False)
    own_chunk = call(
        gate_kernel,
        [],
        [routed.reshape(CHUNK, 2 * HD), *query_pieces[1:]],
        [((CHUNK, 2 * HD), jnp.bfloat16)],
        "gate",
        {0: 0},
        staged=(1, 2, 3),
        anchors=(1, 2, 3),
    )[0]
    qg = call(
        pack_kernel,
        [],
        query_pieces,
        [((PLACES, 2, GROUP, ROWS, HD), jnp.bfloat16)],
        "pack_heads",
        scratch=[pltpu.SemaphoreType.DMA((PLACES,))],
        staged=ALL,
        anchors=ALL,
    )[0]

    chunks = [own_chunk] + [
        lax.ppermute(own_chunk, "cz", swap_pairs(other)) for other in range(1, NZ)
    ]
    stats, kept = None, [None] * NZ
    for other in (0, 1, 3):
        stats, kept[other] = first_pass(scalars, qg, chunks[other], other, stats)
    stats, query_acc, part = bridge_pass(scalars, qg, chunks[2], 2, stats)

    returned = [lax.ppermute(part, "cz", swap_pairs(2))]
    for other in (3, 1):
        query_acc, part = second_pass(
            scalars, qg, chunks[other], kept[other], stats, query_acc
        )
        returned.append(lax.ppermute(part, "cz", swap_pairs(other)))
    last = (scalars, qg, chunks[0], kept[0], stats, query_acc)
    odd, own_part = second_pass(*last, (1, 3))
    even, own_part = second_pass(*last, (0, 2), (own_part, returned[0]))
    query_back = [even[0:1]] + [
        lax.ppermute(piece, "cy", shift_pairs(NY, -shift))
        for shift, piece in ((1, odd[0]), (2, even[1]), (3, odd[1]))
    ]
    page_parts = call(
        sum_kernel,
        [y],
        [own_part, returned[1], returned[2]],
        [((NY, rows, 2 * HD), jnp.bfloat16)],
        "sum_parts",
        hbm=True,
    )[0]
    page_back = lax.all_to_all(page_parts, "cy", 0, 0, tiled=False)
    query_grad, mark = join(
        join_kernel, [y], query_back, (ROWS, HQ * HD), jnp.bfloat16, "join_heads", True
    )
    (cache_grad,) = join(
        join_pages_kernel, [], [page_back, mark], (rows, 2 * HALF), jnp.float32, "join_pages"
    )
    return (
        query_grad.reshape(1, ROWS, HQ * HD),
        cache_grad.reshape(1, SLOTS, 1, PAGE, 2 * HALF),
    )


def solution(mesh):
    split = Mesh(mesh.devices.reshape(NZ, NY, 4, 2, 2), ("cz", "cy") + TRAJ)
    ctx = ("cz", "cy")
    placed = (
        P(TRAJ, ctx, None),
        P(TRAJ, ctx, None),
        P(TRAJ, None, ctx, None, None),
        P(),
        P(),
    )
    return jax.shard_map(
        body,
        mesh=split,
        in_specs=placed,
        out_specs=(P(TRAJ, ctx, None), P(TRAJ, None, ctx, None, None)),
        check_vma=False,
    )
```
